32 devices in a mesh: expert: 8 (over y, x, core), dp: 4 (over z).
Axes of the slice: x: 2, y: 2, z: 4, core: 2. Of those that a mesh axis runs over, the one named last changes fastest.
Arguments:
- tokens: bfloat16 [512, 2048], P(('dp', 'expert')), may hold values from -6 to 6
- cotangent: bfloat16 [512, 8, 384], P(('dp', 'expert')), may hold values from -1 to 1
- expert_ids: int32 [512, 8], P(('dp', 'expert')), may hold values from 0 to 31, all different within a row; in each aligned block of 16 rows (0 to 15, 16 to 31, ...) at most 5 rows name the same one
- placement: int32 [64], replicated, may hold values from 0 to 31, as said below
- master: float32 [32, 1572864], P(None, ('dp', 'expert')), may hold values from -0.125 to 0.125
- first_moment: float32 [32, 1572864], P(None, ('dp', 'expert')), may hold values from -12 to 12
- second_moment: float32 [32, 1572864], P(None, ('dp', 'expert')), may hold values from 1 to 30
Outputs:
- new_master: float32 [32, 1572864], P(None, ('dp', 'expert'))
- new_first: float32 [32, 1572864], P(None, ('dp', 'expert'))
- new_second: float32 [32, 1572864], P(None, ('dp', 'expert'))
- replica_grad: float32 [64, 384, 4096], P('expert', 'dp')
The draws below stay inside these ranges and needn't reach their ends.
Inputs may be any that keep to these rules, and one draw needn't show every extreme that they name: `expert_ids`: among the tokens of one device no expert is named more than 5 times; some device names some expert exactly 5 times. `placement`: every one of the 32 experts holds at least one of the 64 slots.
All inputs are finite; a program needn't handle non-finite values.
Results may differ from the reference program's by a relative error of at most 0.017.
Values may be sent and summed in bfloat16 or wider, within the bound.
A program may use at most 192 MiB of HBM per device.

```python
import math
import jax
import jax.numpy as jnp
import numpy as np
from jax import lax

D = 2048
FF = 384
EXP = 32
TOP = 8
TOK_DEV = 16
MOST = 5
SLOTS = 64
TOKENS = 512
N_EXPERT = 8
N_DP = 4


def draw_placement(key, part):
    first_key = jax.random.fold_in(key, 11)
    second_key = jax.random.fold_in(key, 12)
    label_key = jax.random.fold_in(key, 13)
    order_key = jax.random.fold_in(key, 14)
    first_pick = jax.random.randint(first_key, (SLOTS - EXP,), 0, EXP)
    second_pick = jax.random.randint(second_key, (SLOTS - EXP,), 0, EXP)
    extra = jnp.minimum(first_pick, second_pick)
    base = jnp.concatenate([jnp.arange(EXP, dtype=jnp.int32), extra.astype(jnp.int32)])
    relabel = jax.random.permutation(label_key, EXP).astype(jnp.int32)
    labelled = relabel[base]
    order = jax.random.permutation(order_key, SLOTS).astype(jnp.int32)
    return labelled[order].astype(jnp.int32)


def level_of(rng, dims, split, smallest, high):
    def one(axis_at, shards_of):
        steps = jax.random.uniform(jax.random.fold_in(jax.random.fold_in(rng, 6), axis_at), (shards_of,), jnp.float32, smallest / len(split), high / len(split))
        return jnp.repeat(jnp.exp(steps), dims[axis_at] // shards_of).reshape((-1,) + (1,) * (len(dims) - axis_at - 1))

    level = one(*split[0])
    for cut in split[1:]:
        level = level * one(*cut)
    return level


def shared_out(own_key, own, number, rows, amount, top, most, lean):
    sequence = jax.random.permutation(own_key, amount)
    crowded, usual = load_shares(amount, rows * top, most, lean, True), load_shares(amount, rows * top, most, lean, False)
    places = jnp.arange(amount)

    def named(tallies, turn):
        used = int((tallies > 0).sum())
        fixed = max(1, used // 4)
        moved = fixed + (places - fixed + turn * (used - fixed)) % max(1, amount - fixed)
        return jnp.zeros((amount,), jnp.int32).at[sequence[jnp.where(places < fixed, places, moved)]].set(jnp.asarray(tallies, jnp.int32))

    tallies = jnp.where(number % 4 == 0, named(crowded, number // 4), named(usual, number - number // 4 - 1))
    mixed = jax.random.permutation(jax.random.fold_in(own, 3), amount)
    giver, sink = mixed[0:amount // 2 * 2:2], mixed[1:amount // 2 * 2:2]
    margin = jnp.minimum(tallies[giver] - 1, most - tallies[sink]) // 2
    margin = jnp.where((giver == sequence[0]) | (sink == sequence[0]) | (tallies[sink] == 0), 0, jnp.maximum(margin, 0))
    moved = jax.random.randint(jax.random.fold_in(own, 4), (amount // 2,), 0, 1 << 20) % (margin + 1)
    tallies = tallies.at[giver].add(-moved).at[sink].add(moved)
    members = jnp.searchsorted(jnp.cumsum(tallies), jnp.arange(rows * top), side="right").astype(jnp.int32)
    listing = members.reshape(top, rows).T
    listing = listing[jax.random.permutation(jax.random.fold_in(own, 1), rows)]
    turn = jax.random.randint(jax.random.fold_in(own, 2), (rows, 1), 0, top)
    return jnp.take_along_axis(listing, (jnp.arange(top)[None, :] + turn) % top, axis=1)


def load_shares(amount, total, limit, skew, full):
    portions = [(1 << 20) // math.isqrt(standing ** skew) + 1 for standing in range(1, amount + 1)]
    largest = limit if full else min(limit, max(-(-total // amount), total * portions[0] // sum(portions)))
    least = 1 if total - largest >= amount - 1 else 0
    given, rest = [largest] + [least] * (amount - 1), total - largest - least * (amount - 1)
    while rest > 0:
        candidates = [i for i in range(1, amount) if given[i] < largest] or [i for i in range(1, amount) if given[i] < limit]
        mass, remaining = sum([portions[i] for i in candidates]), rest
        for i in candidates:
            addition = min(limit - given[i], max(1, remaining * portions[i] // mass), rest)
            given[i] = given[i] + addition
            rest = rest - addition
    return np.array(given)


def scatter_about(key, shape, scale, limit, split=(), kind=jnp.bfloat16):
    array = scale * jax.random.normal(key, shape, jnp.float32)
    if split:
        array = array * level_of(key, shape, split, -0.22, 0.18)
    return jnp.clip(array, -limit, limit).astype(kind)


def setup_inputs(seed: int = 0) -> dict:
    arg_keys = jax.random.split(jax.random.key(seed), 8)
    tokens = scatter_about(arg_keys[0], (TOKENS, D), 1.0, 6.0, ((0, 32),))
    cotangent = scatter_about(arg_keys[1], (TOKENS, TOP, FF), 0.125, 1.0, ((0, 32),))
    expert_ids_keys = jax.random.split(jax.random.fold_in(arg_keys[2], 1), TOKENS // TOK_DEV)
    expert_ids_turns = jax.random.permutation(jax.random.fold_in(arg_keys[2], 3), TOKENS // TOK_DEV)
    expert_ids = jax.vmap(lambda own, number: shared_out(jax.random.fold_in(arg_keys[2], 2), own, number, TOK_DEV, EXP, TOP, MOST, 2))(expert_ids_keys, expert_ids_turns).reshape((TOKENS, TOP))
    placement = draw_placement(jax.random.fold_in(arg_keys[7], 71), 0)
    master = scatter_about(arg_keys[4], (EXP, FF * 2 * D), D ** -0.5, 0.125, ((1, 32),), jnp.float32)
    first_moment = scatter_about(arg_keys[5], (EXP, FF * 2 * D), 2.0, 12.0, ((1, 32),), jnp.float32)
    second_moment = jnp.clip(jnp.exp(math.log(30.0) - 3.4011974 * jax.random.uniform(arg_keys[6], (EXP, FF * 2 * D), jnp.float32) ** level_of(arg_keys[6], (EXP, FF * 2 * D), ((1, 32),), -0.2, 0.2)), 1.0, 30.0)
    return {"tokens": tokens, "cotangent": cotangent, "expert_ids": expert_ids, "placement": placement, "master": master, "first_moment": first_moment, "second_moment": second_moment}


beta_first = 0.9
beta_second = 0.95
learning_rate = 0.01
decay_rate = 0.1
epsilon = 1e-08
adam_steps = 20.0

def adamw_update(master, first_moment, second_moment, grads):
    new_first = beta_first * first_moment + (1.0 - beta_first) * grads
    new_second = beta_second * second_moment + (1.0 - beta_second) * grads * grads
    corr_first = 1.0 - beta_first ** adam_steps
    corr_second = 1.0 - beta_second ** adam_steps
    update = new_first / corr_first / (jnp.sqrt(new_second / corr_second) + epsilon) + decay_rate * master
    return (master - learning_rate * update, new_first, new_second)

def swiglu_grads(rows_x, rows_dh, w_gate, w_up):
    gate_value = jnp.dot(rows_x, w_gate.T, preferred_element_type=jnp.float32)
    up_value = jnp.dot(rows_x, w_up.T, preferred_element_type=jnp.float32)
    sigmoid_value = jax.nn.sigmoid(gate_value)
    activation = gate_value * sigmoid_value
    derivative = sigmoid_value * (1.0 + gate_value * (1.0 - sigmoid_value))
    d_gate = (rows_dh * up_value * derivative).astype(jnp.bfloat16)
    d_up = (rows_dh * activation).astype(jnp.bfloat16)
    grad_gate = jnp.dot(d_gate.T, rows_x, preferred_element_type=jnp.float32)
    grad_up = jnp.dot(d_up.T, rows_x, preferred_element_type=jnp.float32)
    return jnp.concatenate([grad_gate, grad_up], axis=1)

def reference(tokens, cotangent, expert_ids, placement, master, first_moment, second_moment):
    assigned = TOK_DEV * TOP
    token_blocks = tokens.reshape(N_DP, N_EXPERT, TOK_DEV, D)
    cot_blocks = cotangent.reshape(N_DP, N_EXPERT, assigned, FF)
    id_blocks = expert_ids.reshape(N_DP, N_EXPERT, assigned)
    expert_range = jnp.arange(EXP, dtype=jnp.int32)
    slot_range = jnp.arange(SLOTS, dtype=jnp.int32)
    replicas = lax.optimization_barrier(jnp.sum((placement[:, None] == expert_range[None, :]).astype(jnp.int32), axis=0))
    earlier_same = (slot_range[:, None] > slot_range[None, :]) & (placement[:, None] == placement[None, :])
    slot_rank = lax.optimization_barrier(jnp.sum(earlier_same.astype(jnp.int32), axis=1))
    expert_hot = id_blocks[..., None] == expert_range
    earlier = jnp.cumsum(expert_hot.astype(jnp.int32), axis=2) - 1
    position = lax.optimization_barrier(jnp.sum(jnp.where(expert_hot, earlier, 0), axis=3))
    weights = master.astype(jnp.bfloat16).reshape(EXP, FF, 2 * D)
    sources = jnp.arange(N_EXPERT, dtype=jnp.int32)
    capacity_range = jnp.arange(MOST, dtype=jnp.int32)

    def slot_step(grads, slot_index):
        expert_index = placement[slot_index]
        chosen = jnp.mod(sources, replicas[expert_index]) == slot_rank[slot_index]
        keep = (id_blocks == expert_index) & chosen[None, :, None]
        slot_rows = (keep[..., None] & (position[..., None] == capacity_range)).astype(jnp.float32)
        replica_weight = weights[expert_index]
        w_gate = replica_weight[:, :D]
        w_up = replica_weight[:, D:]

        def dp_step(total, dp_index):
            picks = slot_rows[dp_index]
            token_picks = lax.optimization_barrier(jnp.sum(picks.reshape(N_EXPERT, TOK_DEV, TOP, MOST), axis=2))
            rows_x = jnp.einsum('stm,std->smd', token_picks, token_blocks[dp_index].astype(jnp.float32))
            rows_x = rows_x.reshape(N_EXPERT * MOST, D).astype(jnp.bfloat16)
            rows_dh = jnp.einsum('sam,saf->smf', picks, cot_blocks[dp_index].astype(jnp.float32))
            rows_dh = rows_dh.reshape(N_EXPERT * MOST, FF).astype(jnp.bfloat16)
            term = swiglu_grads(rows_x, rows_dh, w_gate, w_up)
            rounded = lax.optimization_barrier(term.astype(jnp.bfloat16)).astype(jnp.float32)
            return (total + rounded, None)
        total, _ = lax.scan(dp_step, jnp.zeros((FF, 2 * D), jnp.float32), jnp.arange(N_DP, dtype=jnp.int32))
        return (grads.at[expert_index].add(total.reshape(FF * 2 * D)), total)
    grads, replica_grad = lax.scan(slot_step, jnp.zeros((EXP, FF * 2 * D), jnp.float32), slot_range)
    new_master, new_first, new_second = adamw_update(master, first_moment, second_moment, grads)
    return (new_master, new_first, new_second, replica_grad)
```

```python
import functools

import jax
import jax.numpy as jnp
from jax import lax
from jax.experimental import pallas as pl
from jax.experimental.pallas import tpu as pltpu
from jax.sharding import PartitionSpec as P

MOST = 5


beta_first = 0.9
beta_second = 0.95
learning_rate = 0.01
decay_rate = 0.1
epsilon = 1e-08
adam_steps = 20.0


def adamw_update(master, first_moment, second_moment, grads):
    new_first = beta_first * first_moment + (1.0 - beta_first) * grads
    new_second = beta_second * second_moment + (1.0 - beta_second) * grads * grads
    corr_first = 1.0 - beta_first**adam_steps
    corr_second = 1.0 - beta_second**adam_steps
    update = (
        new_first / corr_first / (jnp.sqrt(new_second / corr_second) + epsilon)
        + decay_rate * master
    )
    return (master - learning_rate * update, new_first, new_second)


def move_weights(tokens, cotangent, expert_ids, placement, master, first_moment, second_moment):
    expert_devices = lax.axis_size("expert")
    source_index = lax.axis_index("expert")
    slot_count = placement.shape[0]
    slot_local = slot_count // expert_devices
    expert_count = master.shape[0]
    shard_width = master.shape[1]
    token_rows = tokens.shape[0]
    model_width = tokens.shape[1]
    top_count = expert_ids.shape[1]
    hidden_width = cotangent.shape[2]
    assigned = token_rows * top_count
    piece_rows = shard_width * expert_devices // (2 * model_width)
    send_total = slot_count * MOST
    expert_range = jnp.arange(expert_count, dtype=jnp.int32)
    slot_range = jnp.arange(slot_count, dtype=jnp.int32)
    slot_hot = placement[:, None] == expert_range[None, :]
    replicas = jnp.sum(slot_hot.astype(jnp.int32), axis=0)
    earlier_same = (slot_range[:, None] > slot_range[None, :]) & (
        placement[:, None] == placement[None, :]
    )
    slot_rank = jnp.sum(earlier_same.astype(jnp.int32), axis=1)
    wanted = jnp.mod(source_index, replicas)
    target_hot = slot_hot & (slot_rank[:, None] == wanted[None, :])
    target_slot = jnp.sum(jnp.where(target_hot, slot_range[:, None], 0), axis=0)
    flat_ids = expert_ids.reshape(assigned)
    expert_hot = flat_ids[:, None] == expert_range[None, :]
    earlier = jnp.cumsum(expert_hot.astype(jnp.int32), axis=0) - 1
    position = jnp.sum(jnp.where(expert_hot, earlier, 0), axis=1)
    destination = jnp.sum(jnp.where(expert_hot, target_slot[None, :], 0), axis=1)
    target_device = destination // slot_local
    local_slot = destination % slot_local
    send_row = (local_slot * expert_devices + target_device) * MOST + position
    copy_range = jnp.arange(assigned, dtype=jnp.int32)
    row_match = jnp.arange(send_total, dtype=jnp.int32)[:, None] == send_row[None, :]
    filled = jnp.any(row_match, axis=1)
    source_copy = jnp.sum(jnp.where(row_match, copy_range[None, :], 0), axis=1)
    gathered_x = jnp.take(tokens, source_copy // top_count, axis=0)
    send_x = jnp.where(filled[:, None], gathered_x, jnp.zeros_like(gathered_x))
    send_x = send_x.reshape(slot_local, expert_devices, MOST, model_width)
    gathered_dh = jnp.take(cotangent.reshape(assigned, hidden_width), source_copy, axis=0)
    send_dh = jnp.where(filled[:, None], gathered_dh, jnp.zeros_like(gathered_dh))
    send_dh = send_dh.reshape(slot_local, expert_devices, MOST, hidden_width)
    piece_expert = placement.reshape(expert_devices, slot_local).T
    send_weight = master[piece_expert].astype(jnp.bfloat16)
    recv_weight = lax.all_to_all(send_weight, "expert", split_axis=1, concat_axis=1, tiled=True)
    recv_x, recv_dh = (
        lax.all_to_all(send_x, "expert", split_axis=1, concat_axis=1, tiled=True),
        lax.all_to_all(send_dh, "expert", split_axis=1, concat_axis=1, tiled=True),
    )
    rows_x = recv_x.reshape(slot_local, expert_devices * MOST, model_width)
    rows_dh = recv_dh.reshape(slot_local, expert_devices * MOST, hidden_width)
    own_piece = recv_weight.reshape(slot_local, piece_rows, 2 * model_width)
    replica = lax.all_gather(own_piece, "dp", axis=1, tiled=True)
    replica_split = replica.reshape(slot_local, hidden_width, 2, model_width)
    both_values = jnp.einsum(
        "lrd,lcgd->lrgc", rows_x, replica_split, preferred_element_type=jnp.float32
    )
    gate_value = both_values[:, :, 0, :]
    up_value = both_values[:, :, 1, :]
    sigmoid_value = jax.nn.sigmoid(gate_value)
    activation = gate_value * sigmoid_value
    derivative = sigmoid_value * (1.0 + gate_value * (1.0 - sigmoid_value))
    d_gate = (rows_dh * up_value * derivative).astype(jnp.bfloat16)
    d_up = (rows_dh * activation).astype(jnp.bfloat16)
    d_both = jnp.stack([d_gate, d_up], axis=2)
    grad_block = jnp.einsum("lrgc,lrd->clgd", d_both, rows_x, preferred_element_type=jnp.float32)
    summed_rows = lax.psum_scatter(
        grad_block.reshape(lax.axis_size("dp") * piece_rows, slot_local, 2 * model_width).astype(
            jnp.bfloat16
        ),
        "dp",
        scatter_dimension=0,
        tiled=True,
    ).astype(jnp.float32)
    replica_grad = jnp.swapaxes(summed_rows, 0, 1)
    outgoing = replica_grad.reshape(slot_local, expert_devices, shard_width)
    incoming = lax.all_to_all(
        outgoing.astype(jnp.bfloat16), "expert", split_axis=1, concat_axis=1, tiled=True
    ).astype(outgoing.dtype)
    by_slot = jnp.swapaxes(incoming, 0, 1).reshape(slot_count, shard_width)
    grads = jnp.dot(
        slot_hot.T.astype(jnp.float32),
        by_slot,
        precision=lax.Precision.HIGHEST,
        preferred_element_type=jnp.float32,
    )
    new_master, new_first, new_second = adamw_update(master, first_moment, second_moment, grads)
    return (new_master, new_first, new_second, replica_grad)


NT = (((1,), (1,)), ((), ()))
VMEM_LIMIT = 56 * 1024 * 1024


def block_count(units, most):
    blocks = 1
    while units % blocks or units // blocks > most:
        blocks += 1
    return blocks


def hidden_kernel(units, top, master, tokens, packed, dense, compact, turned):
    step = pl.program_id(0)
    experts = master.shape[0]
    width = tokens.shape[1]
    total = tokens.shape[0]
    here = master.shape[1] // (2 * width)

    @pl.when(step == 0)
    def _():
        turned[...] = packed[...].astype(jnp.float32).T

    names = turned[units * top : (units + 1) * top, :]
    expert_row = lax.broadcasted_iota(jnp.int32, (experts, total), 0).astype(jnp.float32)
    hot = [(names[a : a + 1, :] == expert_row).astype(jnp.float32) for a in range(top)]
    weights = jnp.concatenate(
        [master[:, c * width : (c + 1) * width].astype(jnp.bfloat16) for c in range(2 * here)],
        axis=0,
    )
    values = lax.dot_general(weights, tokens[...], NT, preferred_element_type=jnp.float32)
    for u in range(here):
        gate = values[2 * u * experts : (2 * u + 1) * experts]
        up = values[(2 * u + 1) * experts : (2 * u + 2) * experts]
        start = pl.multiple_of((step * here + u) * top, top)
        cot_rows = turned[pl.ds(start, top), :]
        cot = cot_rows[0:1, :] * hot[0]
        for a in range(1, top):
            cot = cot + cot_rows[a : a + 1, :] * hot[a]
        sig = 1.0 / (1.0 + jnp.exp(-gate))
        d_gate = cot * up * (sig * (1.0 + gate * (1.0 - sig)))
        d_up = cot * (gate * sig)
        dense[2 * u * experts : (2 * u + 1) * experts, :] = d_gate.astype(jnp.bfloat16)
        dense[(2 * u + 1) * experts : (2 * u + 2) * experts, :] = d_up.astype(jnp.bfloat16)
        picked = [
            jnp.sum(d * hot[a], axis=0, keepdims=True) for d in (d_gate, d_up) for a in range(top)
        ]
        compact[2 * u * top : (2 * u + 2) * top, :] = jnp.concatenate(picked, axis=0).astype(
            jnp.bfloat16
        )


def update_kernel(dense, tokens, master, first, second, new_master, new_first, new_second):
    experts = master.shape[0]
    width = tokens.shape[1]
    grads = jnp.dot(dense[...], tokens[...], preferred_element_type=jnp.float32)
    for c in range(master.shape[1] // width):
        cols = slice(c * width, (c + 1) * width)
        results = adamw_update(
            master[:, cols],
            first[:, cols],
            second[:, cols],
            grads[c * experts : (c + 1) * experts],
        )
        new_master[:, cols], new_first[:, cols], new_second[:, cols] = results


def replica_kernel(top, mask, spread, tokens, out, fold):
    width = tokens.shape[1]
    units = out.shape[1]
    rows = spread.shape[0]

    @pl.when(pl.program_id(0) == 0)
    def _():
        out_row = lax.broadcasted_iota(jnp.int32, fold.shape, 0)
        in_row = lax.broadcasted_iota(jnp.int32, fold.shape, 1) // top
        wanted = (in_row % 2) * units + in_row // 2
        fold[...] = (out_row == wanted).astype(jnp.bfloat16)

    both = jnp.concatenate([mask[0], mask[0]], axis=0)
    masked = spread[...].reshape(rows // (2 * top), 2 * top, -1) * both[None]
    chosen = jnp.dot(
        fold[...], masked.reshape(rows, -1), preferred_element_type=jnp.float32
    ).astype(jnp.bfloat16)
    grad = jnp.dot(chosen, tokens[...], preferred_element_type=jnp.float32)
    out[0, :, :width] = grad[:units]
    out[0, :, width:] = grad[units:]


def params():
    return pltpu.CompilerParams(
        dimension_semantics=("arbitrary",), vmem_limit_bytes=VMEM_LIMIT
    )


def hidden_grads(units, top, master, tokens, packed):
    experts, shard = master.shape
    total = tokens.shape[0]
    blocks = block_count(units, 3)
    here = units // blocks
    return pl.pallas_call(
        functools.partial(hidden_kernel, units, top),
        grid=(blocks,),
        in_specs=[
            pl.BlockSpec((experts, shard // blocks), lambda i: (0, i)),
            pl.BlockSpec(tokens.shape, lambda i: (0, 0)),
            pl.BlockSpec(packed.shape, lambda i: (0, 0)),
        ],
        out_specs=[
            pl.BlockSpec((2 * here * experts, total), lambda i: (i, 0)),
            pl.BlockSpec((2 * here * top, total), lambda i: (i, 0)),
        ],
        out_shape=[
            jax.ShapeDtypeStruct((2 * units * experts, total), jnp.bfloat16),
            jax.ShapeDtypeStruct((2 * units * top, total), jnp.bfloat16),
        ],
        scratch_shapes=[pltpu.VMEM((packed.shape[1], total), jnp.float32)],
        compiler_params=params(),
        name="hidden_grads",
    )(master, tokens, packed)


def update_shards(units, dense, tokens, master, first, second):
    experts, shard = master.shape
    total = tokens.shape[0]
    blocks = block_count(units, 2)
    state = pl.BlockSpec((experts, shard // blocks), lambda i: (0, i))
    return pl.pallas_call(
        update_kernel,
        grid=(blocks,),
        in_specs=[
            pl.BlockSpec((dense.shape[0] // blocks, total), lambda i: (i, 0)),
            pl.BlockSpec(tokens.shape, lambda i: (0, 0)),
            state,
            state,
            state,
        ],
        out_specs=[state] * 3,
        out_shape=[jax.ShapeDtypeStruct(master.shape, jnp.float32)] * 3,
        compiler_params=params(),
        cost_estimate=pl.CostEstimate(
            flops=2 * dense.shape[0] * total * tokens.shape[1],
            bytes_accessed=24 * master.size,
            transcendentals=0,
        ),
        name="update_shards",
    )(dense, tokens, master, first, second)


def replica_grads(units, top, mask, spread, tokens):
    slots, _, total = mask.shape
    width = tokens.shape[1]
    return pl.pallas_call(
        functools.partial(replica_kernel, top),
        grid=(slots,),
        in_specs=[
            pl.BlockSpec((1, top, total), lambda i: (i, 0, 0)),
            pl.BlockSpec(spread.shape, lambda i: (0, 0)),
            pl.BlockSpec(tokens.shape, lambda i: (0, 0)),
        ],
        out_specs=pl.BlockSpec((1, units, 2 * width), lambda i: (i, 0, 0)),
        out_shape=jax.ShapeDtypeStruct((slots, units, 2 * width), jnp.float32),
        scratch_shapes=[pltpu.VMEM((2 * units, spread.shape[0]), jnp.bfloat16)],
        compiler_params=params(),
        name="replica_grads",
    )(mask, spread, tokens)


def slot_masks(placement, names, expert_count, slot_local, token_rows):
    expert_devices = lax.axis_size("expert")
    slot_count = placement.shape[0]
    slot_range = jnp.arange(slot_count, dtype=jnp.int32)
    same = placement[:, None] == placement[None, :]
    replicas = jnp.sum(same.astype(jnp.int32), axis=1)
    earlier = same & (slot_range[:, None] > slot_range[None, :])
    rank = jnp.sum(earlier.astype(jnp.int32), axis=1)
    first_slot = lax.axis_index("expert") * slot_local
    own = lambda values: lax.dynamic_slice_in_dim(values, first_slot, slot_local)
    source = jnp.arange(names.shape[1], dtype=jnp.int32) // token_rows % expert_devices
    chosen = source[None, :] % own(replicas)[:, None] == own(rank)[:, None]
    held = own(placement)[:, None, None].astype(names.dtype) == names[None]
    return (held & chosen[:, None, :]).astype(jnp.bfloat16)


def move_tokens(tokens, cotangent, expert_ids, placement, master, first_moment, second_moment):
    axes = ("dp", "expert")
    devices = lax.axis_size("dp") * lax.axis_size("expert")
    token_rows, width = tokens.shape
    top, hidden = cotangent.shape[1:]
    experts, shard = master.shape
    units = shard // (2 * width)
    slot_local = placement.shape[0] // lax.axis_size("expert")
    pieces = cotangent.reshape(token_rows, top, devices, units).transpose(2, 0, 3, 1)
    pieces = pieces.reshape(devices, token_rows, units * top)
    names = jnp.broadcast_to(expert_ids.astype(jnp.bfloat16)[None], (devices, token_rows, top))
    lanes = (units + 1) * top
    packed = jnp.concatenate([pieces, names], axis=2)
    packed = jnp.pad(packed, ((0, 0), (0, 0), (0, -lanes % 128)))
    packed = lax.all_to_all(packed, axes, split_axis=0, concat_axis=0, tiled=True)
    packed = packed.reshape(devices * token_rows, -1)
    all_tokens = lax.all_gather(tokens, axes, axis=0, tiled=True)
    dense, compact = hidden_grads(units, top, master, all_tokens, packed)
    spread = lax.all_gather(compact, "expert", axis=0, tiled=True)
    states = update_shards(units, dense, all_tokens, master, first_moment, second_moment)
    all_names = packed[:, units * top : lanes].T
    mask = slot_masks(placement, all_names, experts, slot_local, token_rows)
    replica_grad = replica_grads(
        units * lax.axis_size("expert"), top, mask, spread, all_tokens
    )
    return (*states, replica_grad)


def local(tokens, cotangent, expert_ids, placement, master, first_moment, second_moment):
    devices = lax.axis_size("dp") * lax.axis_size("expert")
    token_values = tokens.size * devices
    weight_values = placement.shape[0] // lax.axis_size("expert") * cotangent.shape[2] * 2 * tokens.shape[1]
    whole_units = master.shape[1] % (2 * tokens.shape[1]) == 0
    few = token_values < weight_values and tokens.shape[0] * devices % 128 == 0
    exact = master.shape[0] <= 256 and tokens.shape[0] % 16 == 0
    plan = move_tokens if whole_units and few and exact else move_weights
    return plan(tokens, cotangent, expert_ids, placement, master, first_moment, second_moment)


def solution(mesh):
    return jax.shard_map(
        local,
        mesh=mesh,
        in_specs=(
            P(("dp", "expert"), None),
            P(("dp", "expert"), None, None),
            P(("dp", "expert"), None),
            P(),
            P(None, ("dp", "expert")),
            P(None, ("dp", "expert")),
            P(None, ("dp", "expert")),
        ),
        out_specs=(
            P(None, ("dp", "expert")),
            P(None, ("dp", "expert")),
            P(None, ("dp", "expert")),
            P("expert", "dp", None),
        ),
        check_vma=False,
    )
```

```python
import functools

import jax
import jax.numpy as jnp
from jax import lax
from jax.experimental import pallas as pl
from jax.experimental.pallas import tpu as pltpu
from jax.sharding import PartitionSpec as P

MOST = 5


beta_first = 0.9
beta_second = 0.95
learning_rate = 0.01
decay_rate = 0.1
epsilon = 1e-08
adam_steps = 20.0


def adamw_update(master, first_moment, second_moment, grads):
    new_first = beta_first * first_moment + (1.0 - beta_first) * grads
    new_second = beta_second * second_moment + (1.0 - beta_second) * grads * grads
    corr_first = 1.0 - beta_first**adam_steps
    corr_second = 1.0 - beta_second**adam_steps
    update = (
        new_first / corr_first / (jnp.sqrt(new_second / corr_second) + epsilon)
        + decay_rate * master
    )
    return (master - learning_rate * update, new_first, new_second)


def move_weights(tokens, cotangent, expert_ids, placement, master, first_moment, second_moment):
    expert_devices = lax.axis_size("expert")
    source_index = lax.axis_index("expert")
    slot_count = placement.shape[0]
    slot_local = slot_count // expert_devices
    expert_count = master.shape[0]
    shard_width = master.shape[1]
    token_rows = tokens.shape[0]
    model_width = tokens.shape[1]
    top_count = expert_ids.shape[1]
    hidden_width = cotangent.shape[2]
    assigned = token_rows * top_count
    piece_rows = shard_width * expert_devices // (2 * model_width)
    send_total = slot_count * MOST
    expert_range = jnp.arange(expert_count, dtype=jnp.int32)
    slot_range = jnp.arange(slot_count, dtype=jnp.int32)
    slot_hot = placement[:, None] == expert_range[None, :]
    replicas = jnp.sum(slot_hot.astype(jnp.int32), axis=0)
    earlier_same = (slot_range[:, None] > slot_range[None, :]) & (
        placement[:, None] == placement[None, :]
    )
    slot_rank = jnp.sum(earlier_same.astype(jnp.int32), axis=1)
    wanted = jnp.mod(source_index, replicas)
    target_hot = slot_hot & (slot_rank[:, None] == wanted[None, :])
    target_slot = jnp.sum(jnp.where(target_hot, slot_range[:, None], 0), axis=0)
    flat_ids = expert_ids.reshape(assigned)
    expert_hot = flat_ids[:, None] == expert_range[None, :]
    earlier = jnp.cumsum(expert_hot.astype(jnp.int32), axis=0) - 1
    position = jnp.sum(jnp.where(expert_hot, earlier, 0), axis=1)
    destination = jnp.sum(jnp.where(expert_hot, target_slot[None, :], 0), axis=1)
    target_device = destination // slot_local
    local_slot = destination % slot_local
    send_row = (local_slot * expert_devices + target_device) * MOST + position
    copy_range = jnp.arange(assigned, dtype=jnp.int32)
    row_match = jnp.arange(send_total, dtype=jnp.int32)[:, None] == send_row[None, :]
    filled = jnp.any(row_match, axis=1)
    source_copy = jnp.sum(jnp.where(row_match, copy_range[None, :], 0), axis=1)
    gathered_x = jnp.take(tokens, source_copy // top_count, axis=0)
    send_x = jnp.where(filled[:, None], gathered_x, jnp.zeros_like(gathered_x))
    send_x = send_x.reshape(slot_local, expert_devices, MOST, model_width)
    gathered_dh = jnp.take(cotangent.reshape(assigned, hidden_width), source_copy, axis=0)
    send_dh = jnp.where(filled[:, None], gathered_dh, jnp.zeros_like(gathered_dh))
    send_dh = send_dh.reshape(slot_local, expert_devices, MOST, hidden_width)
    piece_expert = placement.reshape(expert_devices, slot_local).T
    send_weight = master[piece_expert].astype(jnp.bfloat16)
    recv_weight = lax.all_to_all(send_weight, "expert", split_axis=1, concat_axis=1, tiled=True)
    recv_x, recv_dh = (
        lax.all_to_all(send_x, "expert", split_axis=1, concat_axis=1, tiled=True),
        lax.all_to_all(send_dh, "expert", split_axis=1, concat_axis=1, tiled=True),
    )
    rows_x = recv_x.reshape(slot_local, expert_devices * MOST, model_width)
    rows_dh = recv_dh.reshape(slot_local, expert_devices * MOST, hidden_width)
    own_piece = recv_weight.reshape(slot_local, piece_rows, 2 * model_width)
    replica = lax.all_gather(own_piece, "dp", axis=1, tiled=True)
    replica_split = replica.reshape(slot_local, hidden_width, 2, model_width)
    both_values = jnp.einsum(
        "lrd,lcgd->lrgc", rows_x, replica_split, preferred_element_type=jnp.float32
    )
    gate_value = both_values[:, :, 0, :]
    up_value = both_values[:, :, 1, :]
    sigmoid_value = jax.nn.sigmoid(gate_value)
    activation = gate_value * sigmoid_value
    derivative = sigmoid_value * (1.0 + gate_value * (1.0 - sigmoid_value))
    d_gate = (rows_dh * up_value * derivative).astype(jnp.bfloat16)
    d_up = (rows_dh * activation).astype(jnp.bfloat16)
    d_both = jnp.stack([d_gate, d_up], axis=2)
    grad_block = jnp.einsum("lrgc,lrd->clgd", d_both, rows_x, preferred_element_type=jnp.float32)
    summed_rows = lax.psum_scatter(
        grad_block.reshape(lax.axis_size("dp") * piece_rows, slot_local, 2 * model_width).astype(
            jnp.bfloat16
        ),
        "dp",
        scatter_dimension=0,
        tiled=True,
    ).astype(jnp.float32)
    replica_grad = jnp.swapaxes(summed_rows, 0, 1)
    outgoing = replica_grad.reshape(slot_local, expert_devices, shard_width)
    incoming = lax.all_to_all(
        outgoing.astype(jnp.bfloat16), "expert", split_axis=1, concat_axis=1, tiled=True
    ).astype(outgoing.dtype)
    by_slot = jnp.swapaxes(incoming, 0, 1).reshape(slot_count, shard_width)
    grads = jnp.dot(
        slot_hot.T.astype(jnp.float32),
        by_slot,
        precision=lax.Precision.HIGHEST,
        preferred_element_type=jnp.float32,
    )
    new_master, new_first, new_second = adamw_update(master, first_moment, second_moment, grads)
    return (new_master, new_first, new_second, replica_grad)


NT = (((1,), (1,)), ((), ()))
VMEM_LIMIT = 56 * 1024 * 1024


def block_count(units, most):
    blocks = 1
    while units % blocks or units // blocks > most:
        blocks += 1
    return blocks


def exchange_kernel(
    units, pad, blocks, tokens, cot, ids, master,
    all_tokens, dense, spread, names,
    held, weights, packed, landed, turned,
    held_sem, own_sem, row_sems, plane_sems, pair_sems, piece_sems, swap_sems, share_sems,
):
    groups, members = lax.axis_size("dp"), lax.axis_size("expert")
    pairs = members // 2
    count = groups * members
    group, member = lax.axis_index("dp"), lax.axis_index("expert")
    pair, half = member // 2, member % 2
    me = group * members + member
    own_rows, width = tokens.shape
    experts, top = master.shape[0], ids.shape[1]
    total = all_tokens.shape[0]
    here = units // blocks
    block_cols = master.shape[1] // blocks

    def device(g, e):
        return {"dp": g, "expert": e}

    def remote(source, target, sems, index, to):
        return pltpu.make_async_remote_copy(
            src_ref=source, dst_ref=target,
            send_sem=sems.at[(0, *index)], recv_sem=sems.at[(1, *index)],
            device_id=to, device_id_type=pl.DeviceIdType.MESH,
        )

    def shard(h, q, c):
        owner = ((group + groups - h) % groups) * members + 2 * ((pair + pairs - q) % pairs) + c
        return all_tokens.at[pl.ds(pl.multiple_of(owner * own_rows, own_rows), own_rows)]

    def along(h):
        to = device((group + h) % groups, member)
        return remote(shard(0, 0, half), shard(0, 0, half), row_sems, (h,), to)

    def across(h, q):
        to = device(group, 2 * ((pair + q) % pairs) + half)
        return remote(shard(h, 0, half), shard(h, 0, half), plane_sems, (h, q), to)

    def sideways(h, q):
        to = device(group, 2 * pair + 1 - half)
        return remote(shard(h, q, half), shard(h, q, half), pair_sems, (h, q), to)

    def piece(step):
        other = (me + step) % count
        source = packed.at[pl.ds(pl.multiple_of(other * pad, pad), pad)]
        target = landed.at[pl.ds(pl.multiple_of(me * pad, pad), pad)]
        return remote(source, target, piece_sems, (step,), device(other // members, other % members))

    share = 2 * here * top

    def part(b, q, c):
        owner = 2 * ((pair + pairs - q) % pairs) + c
        start = owner * (blocks * share) + b * share
        return spread.at[pl.ds(pl.multiple_of(start, share), share)]

    def swap(b, q):
        to = device(group, 2 * ((pair + q) % pairs) + half)
        return remote(part(b, 0, half), part(b, 0, half), swap_sems, (b, q), to)

    def pass_on(b, q):
        to = device(group, 2 * pair + 1 - half)
        return remote(part(b, q, half), part(b, q, half), share_sems, (b, q), to)

    loads = []
    for b in range(blocks):
        cols = pl.ds(b * block_cols, block_cols)
        loads.append(pltpu.make_async_copy(master.at[:, cols], held.at[:, cols], held_sem.at[b]))
    all_tokens[pl.ds(pl.multiple_of(me * own_rows, own_rows), own_rows), :] = tokens[...]

    barrier = pltpu.get_barrier_semaphore()

    @pl.loop(1, count)
    def _(step):
        other = (me + step) % count
        pl.semaphore_signal(
            barrier, inc=1, device_id=device(other // members, other % members),
            device_id_type=pl.DeviceIdType.MESH,
        )

    for load in loads:
        load.start()
    pl.semaphore_wait(barrier, count - 1)

    for h in range(1, groups):
        along(h).start()
    for q in range(1, pairs):
        across(0, q).start()
    sideways(0, 0).start()

    out_row = lax.broadcasted_iota(jnp.int32, (count * pad, cot.shape[1]), 0)
    in_col = lax.broadcasted_iota(jnp.int32, (count * pad, cot.shape[1]), 1)
    wanted = (out_row // pad) * units + out_row % pad
    pick = ((in_col == wanted) & (out_row % pad < units)).astype(jnp.bfloat16)
    turned_cot = lax.dot_general(pick, cot[...], NT, preferred_element_type=jnp.float32)
    lane = lax.broadcasted_iota(jnp.int32, (own_rows, own_rows * top), 1)
    row = lax.broadcasted_iota(jnp.int32, (own_rows, own_rows * top), 0)
    flat = jnp.zeros((own_rows, own_rows * top), jnp.float32)
    numbers = ids[...].astype(jnp.float32)
    for a in range(top):
        flat = flat + jnp.where(lane == row * top + a, numbers[:, a : a + 1], 0.0)
    flat = jnp.sum(flat, axis=0, keepdims=True)
    kind = lax.broadcasted_iota(jnp.int32, turned_cot.shape, 0) % pad
    packed[...] = jnp.where(kind == units, flat, turned_cot).astype(jnp.bfloat16)

    @pl.loop(1, count)
    def _(step):
        piece(step).start()

    mine = pl.ds(pl.multiple_of(me * pad, pad), pad)
    own = pltpu.make_async_copy(packed.at[mine], landed.at[mine], own_sem.at[0])
    own.start()

    for h in range(1, groups):
        along(h).wait_recv()
        for q in range(1, pairs):
            across(h, q).start()
        sideways(h, 0).start()

    for b in range(blocks):
        loads[b].wait()
        for c in range(2 * b * here, 2 * (b + 1) * here):
            weights[c * experts : (c + 1) * experts, :] = held[
                :, c * width : (c + 1) * width
            ].astype(jnp.bfloat16)

    for h in range(groups):
        for q in range(1, pairs):
            across(h, q).wait_recv()
            sideways(h, q).start()

    own.wait()

    @pl.loop(1, count)
    def _(step):
        piece(step).wait()

    from_row = lax.broadcasted_iota(jnp.int32, (own_rows * top, total), 0)
    to_col = lax.broadcasted_iota(jnp.int32, (own_rows * top, total), 1) % own_rows
    source_row = lax.broadcasted_iota(jnp.int32, (count * pad, total), 0) // pad
    source_col = lax.broadcasted_iota(jnp.int32, (count * pad, total), 1) // own_rows
    same = (source_row == source_col).astype(jnp.float32)
    unit_row = lax.broadcasted_iota(jnp.int32, (pad, count * pad), 0)
    unit_col = lax.broadcasted_iota(jnp.int32, (pad, count * pad), 1) % pad
    gather = (unit_row == unit_col).astype(jnp.bfloat16)
    for a in range(top):
        lanes = (from_row == to_col * top + a).astype(jnp.bfloat16)
        wide = jnp.dot(landed[...], lanes, preferred_element_type=jnp.float32) * same
        turned[a] = jnp.dot(
            gather, wide.astype(jnp.bfloat16), preferred_element_type=jnp.float32
        )

    for h in range(groups):
        for q in range(pairs):
            sideways(h, q).wait_recv()

    expert_row = lax.broadcasted_iota(jnp.int32, (experts, total), 0).astype(jnp.float32)
    for a in range(top):
        names[a : a + 1, :] = turned[a, units : units + 1, :]

    @pl.loop(0, blocks)
    def _(b):
        first = pl.multiple_of(b * (2 * here * experts), 2 * here * experts)
        values = lax.dot_general(
            weights[pl.ds(first, 2 * here * experts), :],
            all_tokens[...],
            NT,
            preferred_element_type=jnp.float32,
        )
        hot = [(names[a : a + 1, :] == expert_row).astype(jnp.float32) for a in range(top)]
        picked = []
        both = []
        for u in range(here):
            gate = values[2 * u * experts : (2 * u + 1) * experts]
            up = values[(2 * u + 1) * experts : (2 * u + 2) * experts]
            cot_dense = turned[0, pl.ds(b * here + u, 1), :] * hot[0]
            for a in range(1, top):
                cot_dense = cot_dense + turned[a, pl.ds(b * here + u, 1), :] * hot[a]
            sig = 1.0 / (1.0 + jnp.exp(-gate))
            d_gate = cot_dense * up * (sig * (1.0 + gate * (1.0 - sig)))
            d_up = cot_dense * (gate * sig)
            both += [d_gate, d_up]
            picked += [
                jnp.sum(d * hot[a], axis=0, keepdims=True)
                for d in (d_gate, d_up)
                for a in range(top)
            ]
        dense[pl.ds(first, 2 * here * experts), :] = jnp.concatenate(both, axis=0).astype(
            jnp.bfloat16
        )
        start = pl.multiple_of(member * (blocks * share) + b * share, share)
        spread[pl.ds(start, share), :] = jnp.concatenate(picked, axis=0).astype(jnp.bfloat16)
        for q in range(1, pairs):
            swap(b, q).start()
        pass_on(b, 0).start()

        @pl.when(b > 0)
        def _():
            for q in range(1, pairs):
                swap(b - 1, q).wait_recv()
                pass_on(b - 1, q).start()

    for q in range(1, pairs):
        swap(blocks - 1, q).wait_recv()
        pass_on(blocks - 1, q).start()

    for h in range(groups):
        if h:
            along(h).wait_send()
        for q in range(pairs):
            if q:
                across(h, q).wait_send()
            sideways(h, q).wait_send()
    for b in range(blocks):
        for q in range(pairs):
            if q:
                swap(b, q).wait_send()
            pass_on(b, q).wait()


def exchange(units, tokens, cotangent, expert_ids, master):
    groups, members = lax.axis_size("dp"), lax.axis_size("expert")
    count = groups * members
    own_rows, width = tokens.shape
    top, hidden = cotangent.shape[1:]
    total = own_rows * count
    experts = master.shape[0]
    pad = -(-(units + 1) // 16) * 16
    blocks = block_count(units, 3)
    dma = pltpu.SemaphoreType.DMA
    vmem = pl.BlockSpec(memory_space=pltpu.VMEM)
    return pl.pallas_call(
        functools.partial(exchange_kernel, units, pad, blocks),
        in_specs=[vmem, vmem, vmem, pl.BlockSpec(memory_space=pl.ANY)],
        out_specs=[vmem] * 4,
        out_shape=[
            jax.ShapeDtypeStruct((total, width), jnp.bfloat16),
            jax.ShapeDtypeStruct((2 * units * experts, total), jnp.bfloat16),
            jax.ShapeDtypeStruct((members * 2 * units * top, total), jnp.bfloat16),
            jax.ShapeDtypeStruct((top, total), jnp.float32),
        ],
        scratch_shapes=[
            pltpu.VMEM(master.shape, jnp.float32),
            pltpu.VMEM((2 * units * experts, width), jnp.bfloat16),
            pltpu.VMEM((count * pad, own_rows * top), jnp.bfloat16),
            pltpu.VMEM((count * pad, own_rows * top), jnp.bfloat16),
            pltpu.VMEM((top, pad, total), jnp.float32),
            dma((blocks,)),
            dma((1,)),
            dma((2, groups)),
            dma((2, groups, members // 2)),
            dma((2, groups, members // 2)),
            dma((2, count)),
            dma((2, blocks, members // 2)),
            dma((2, blocks, members // 2)),
        ],
        compiler_params=pltpu.CompilerParams(
            collective_id=0, has_side_effects=True, vmem_limit_bytes=VMEM_LIMIT
        ),
        name="exchange",
    )(tokens, cotangent.reshape(own_rows * top, hidden), expert_ids, master)


def finish_kernel(
    top, mask, spread, dense, tokens, master, first, second,
    new_master, new_first, new_second, out, fold,
):
    experts = master.shape[0]
    width = tokens.shape[1]
    units = out.shape[1]
    rows = spread.shape[0]

    @pl.when(pl.program_id(0) == 0)
    def _():
        out_row = lax.broadcasted_iota(jnp.int32, fold.shape, 0)
        in_row = lax.broadcasted_iota(jnp.int32, fold.shape, 1) // top
        wanted = (in_row % 2) * units + in_row // 2
        fold[...] = (out_row == wanted).astype(jnp.bfloat16)

    both = jnp.concatenate([mask[0], mask[0]], axis=0)
    masked = spread[...].reshape(rows // (2 * top), 2 * top, -1) * both[None]
    chosen = jnp.dot(
        fold[...], masked.reshape(rows, -1), preferred_element_type=jnp.float32
    ).astype(jnp.bfloat16)
    grad = jnp.dot(chosen, tokens[...], preferred_element_type=jnp.float32)
    out[0, :, :width] = grad[:units]
    out[0, :, width:] = grad[units:]
    grads = jnp.dot(dense[...], tokens[...], preferred_element_type=jnp.float32)
    for c in range(master.shape[1] // width):
        cols = slice(c * width, (c + 1) * width)
        results = adamw_update(
            master[:, cols],
            first[:, cols],
            second[:, cols],
            grads[c * experts : (c + 1) * experts],
        )
        new_master[:, cols], new_first[:, cols], new_second[:, cols] = results


def finish(units, top, mask, spread, dense, tokens, master, first, second):
    slots, _, total = mask.shape
    experts, shard = master.shape
    width = tokens.shape[1]
    state = pl.BlockSpec((experts, shard // slots), lambda i: (0, i))
    return pl.pallas_call(
        functools.partial(finish_kernel, top),
        grid=(slots,),
        in_specs=[
            pl.BlockSpec((1, top, total), lambda i: (i, 0, 0)),
            pl.BlockSpec(spread.shape, lambda i: (0, 0)),
            pl.BlockSpec((dense.shape[0] // slots, total), lambda i: (i, 0)),
            pl.BlockSpec(tokens.shape, lambda i: (0, 0)),
            state,
            state,
            state,
        ],
        out_specs=[state] * 3 + [pl.BlockSpec((1, units, 2 * width), lambda i: (i, 0, 0))],
        out_shape=[jax.ShapeDtypeStruct(master.shape, jnp.float32)] * 3
        + [jax.ShapeDtypeStruct((slots, units, 2 * width), jnp.float32)],
        scratch_shapes=[pltpu.VMEM((2 * units, spread.shape[0]), jnp.bfloat16)],
        compiler_params=pltpu.CompilerParams(
            dimension_semantics=("arbitrary",), vmem_limit_bytes=VMEM_LIMIT
        ),
        name="finish",
    )(mask, spread, dense, tokens, master, first, second)


def slot_masks(placement, names, slot_local, token_rows):
    expert_devices = lax.axis_size("expert")
    slot_count = placement.shape[0]
    slot_range = jnp.arange(slot_count, dtype=jnp.int32)
    same = placement[:, None] == placement[None, :]
    replicas = jnp.sum(same.astype(jnp.int32), axis=1)
    earlier = same & (slot_range[:, None] > slot_range[None, :])
    rank = jnp.sum(earlier.astype(jnp.int32), axis=1)
    first_slot = lax.axis_index("expert") * slot_local
    own = lambda values: lax.dynamic_slice_in_dim(values, first_slot, slot_local)
    source = jnp.arange(names.shape[1], dtype=jnp.int32) // token_rows % expert_devices
    chosen = source[None, :] % own(replicas)[:, None] == own(rank)[:, None]
    held = own(placement)[:, None, None].astype(names.dtype) == names[None]
    return (held & chosen[:, None, :]).astype(jnp.bfloat16)


def move_tokens(tokens, cotangent, expert_ids, placement, master, first_moment, second_moment):
    members = lax.axis_size("expert")
    top = cotangent.shape[1]
    units = master.shape[1] // (2 * tokens.shape[1])
    slot_local = placement.shape[0] // members
    all_tokens, dense, spread, names = exchange(units, tokens, cotangent, expert_ids, master)
    mask = slot_masks(placement, names, slot_local, tokens.shape[0])
    return tuple(
        finish(
            units * members, top, mask, spread, dense, all_tokens,
            master, first_moment, second_moment,
        )
    )


def local(tokens, cotangent, expert_ids, placement, master, first_moment, second_moment):
    devices = lax.axis_size("dp") * lax.axis_size("expert")
    token_values = tokens.size * devices
    weight_values = placement.shape[0] // lax.axis_size("expert") * cotangent.shape[2] * 2 * tokens.shape[1]
    whole_units = master.shape[1] % (2 * tokens.shape[1]) == 0
    few = token_values < weight_values and tokens.shape[0] * devices % 128 == 0
    exact = master.shape[0] <= 256 and tokens.shape[0] % 16 == 0 and cotangent.shape[1] % 8 == 0
    slot_local = placement.shape[0] // lax.axis_size("expert")
    even = lax.axis_size("expert") % 2 == 0
    even = even and master.shape[1] // tokens.shape[1] % slot_local == 0
    plan = move_tokens if whole_units and few and exact and even else move_weights
    return plan(tokens, cotangent, expert_ids, placement, master, first_moment, second_moment)


def solution(mesh):
    return jax.shard_map(
        local,
        mesh=mesh,
        in_specs=(
            P(("dp", "expert"), None),
            P(("dp", "expert"), None, None),
            P(("dp", "expert"), None),
            P(),
            P(None, ("dp", "expert")),
            P(None, ("dp", "expert")),
            P(None, ("dp", "expert")),
        ),
        out_specs=(
            P(None, ("dp", "expert")),
            P(None, ("dp", "expert")),
            P(None, ("dp", "expert")),
            P("expert", "dp", None),
        ),
        check_vma=False,
    )
```

```python
import functools

import jax
import jax.numpy as jnp
from jax import lax
from jax.experimental import pallas as pl
from jax.experimental.pallas import tpu as pltpu
from jax.sharding import PartitionSpec as P

MOST = 5


beta_first = 0.9
beta_second = 0.95
learning_rate = 0.01
decay_rate = 0.1
epsilon = 1e-08
adam_steps = 20.0


def adamw_update(master, first_moment, second_moment, grads):
    new_first = beta_first * first_moment + (1.0 - beta_first) * grads
    new_second = beta_second * second_moment + (1.0 - beta_second) * grads * grads
    corr_first = 1.0 - beta_first**adam_steps
    corr_second = 1.0 - beta_second**adam_steps
    update = (
        new_first / corr_first / (jnp.sqrt(new_second / corr_second) + epsilon)
        + decay_rate * master
    )
    return (master - learning_rate * update, new_first, new_second)


def move_weights(tokens, cotangent, expert_ids, placement, master, first_moment, second_moment):
    expert_devices = lax.axis_size("expert")
    source_index = lax.axis_index("expert")
    slot_count = placement.shape[0]
    slot_local = slot_count // expert_devices
    expert_count = master.shape[0]
    shard_width = master.shape[1]
    token_rows = tokens.shape[0]
    model_width = tokens.shape[1]
    top_count = expert_ids.shape[1]
    hidden_width = cotangent.shape[2]
    assigned = token_rows * top_count
    piece_rows = shard_width * expert_devices // (2 * model_width)
    send_total = slot_count * MOST
    expert_range = jnp.arange(expert_count, dtype=jnp.int32)
    slot_range = jnp.arange(slot_count, dtype=jnp.int32)
    slot_hot = placement[:, None] == expert_range[None, :]
    replicas = jnp.sum(slot_hot.astype(jnp.int32), axis=0)
    earlier_same = (slot_range[:, None] > slot_range[None, :]) & (
        placement[:, None] == placement[None, :]
    )
    slot_rank = jnp.sum(earlier_same.astype(jnp.int32), axis=1)
    wanted = jnp.mod(source_index, replicas)
    target_hot = slot_hot & (slot_rank[:, None] == wanted[None, :])
    target_slot = jnp.sum(jnp.where(target_hot, slot_range[:, None], 0), axis=0)
    flat_ids = expert_ids.reshape(assigned)
    expert_hot = flat_ids[:, None] == expert_range[None, :]
    earlier = jnp.cumsum(expert_hot.astype(jnp.int32), axis=0) - 1
    position = jnp.sum(jnp.where(expert_hot, earlier, 0), axis=1)
    destination = jnp.sum(jnp.where(expert_hot, target_slot[None, :], 0), axis=1)
    target_device = destination // slot_local
    local_slot = destination % slot_local
    send_row = (local_slot * expert_devices + target_device) * MOST + position
    copy_range = jnp.arange(assigned, dtype=jnp.int32)
    row_match = jnp.arange(send_total, dtype=jnp.int32)[:, None] == send_row[None, :]
    filled = jnp.any(row_match, axis=1)
    source_copy = jnp.sum(jnp.where(row_match, copy_range[None, :], 0), axis=1)
    gathered_x = jnp.take(tokens, source_copy // top_count, axis=0)
    send_x = jnp.where(filled[:, None], gathered_x, jnp.zeros_like(gathered_x))
    send_x = send_x.reshape(slot_local, expert_devices, MOST, model_width)
    gathered_dh = jnp.take(cotangent.reshape(assigned, hidden_width), source_copy, axis=0)
    send_dh = jnp.where(filled[:, None], gathered_dh, jnp.zeros_like(gathered_dh))
    send_dh = send_dh.reshape(slot_local, expert_devices, MOST, hidden_width)
    piece_expert = placement.reshape(expert_devices, slot_local).T
    send_weight = master[piece_expert].astype(jnp.bfloat16)
    recv_weight = lax.all_to_all(send_weight, "expert", split_axis=1, concat_axis=1, tiled=True)
    recv_x, recv_dh = (
        lax.all_to_all(send_x, "expert", split_axis=1, concat_axis=1, tiled=True),
        lax.all_to_all(send_dh, "expert", split_axis=1, concat_axis=1, tiled=True),
    )
    rows_x = recv_x.reshape(slot_local, expert_devices * MOST, model_width)
    rows_dh = recv_dh.reshape(slot_local, expert_devices * MOST, hidden_width)
    own_piece = recv_weight.reshape(slot_local, piece_rows, 2 * model_width)
    replica = lax.all_gather(own_piece, "dp", axis=1, tiled=True)
    replica_split = replica.reshape(slot_local, hidden_width, 2, model_width)
    both_values = jnp.einsum(
        "lrd,lcgd->lrgc", rows_x, replica_split, preferred_element_type=jnp.float32
    )
    gate_value = both_values[:, :, 0, :]
    up_value = both_values[:, :, 1, :]
    sigmoid_value = jax.nn.sigmoid(gate_value)
    activation = gate_value * sigmoid_value
    derivative = sigmoid_value * (1.0 + gate_value * (1.0 - sigmoid_value))
    d_gate = (rows_dh * up_value * derivative).astype(jnp.bfloat16)
    d_up = (rows_dh * activation).astype(jnp.bfloat16)
    d_both = jnp.stack([d_gate, d_up], axis=2)
    grad_block = jnp.einsum("lrgc,lrd->clgd", d_both, rows_x, preferred_element_type=jnp.float32)
    summed_rows = lax.psum_scatter(
        grad_block.reshape(lax.axis_size("dp") * piece_rows, slot_local, 2 * model_width).astype(
            jnp.bfloat16
        ),
        "dp",
        scatter_dimension=0,
        tiled=True,
    ).astype(jnp.float32)
    replica_grad = jnp.swapaxes(summed_rows, 0, 1)
    outgoing = replica_grad.reshape(slot_local, expert_devices, shard_width)
    incoming = lax.all_to_all(
        outgoing.astype(jnp.bfloat16), "expert", split_axis=1, concat_axis=1, tiled=True
    ).astype(outgoing.dtype)
    by_slot = jnp.swapaxes(incoming, 0, 1).reshape(slot_count, shard_width)
    grads = jnp.dot(
        slot_hot.T.astype(jnp.float32),
        by_slot,
        precision=lax.Precision.HIGHEST,
        preferred_element_type=jnp.float32,
    )
    new_master, new_first, new_second = adamw_update(master, first_moment, second_moment, grads)
    return (new_master, new_first, new_second, replica_grad)


NT = (((1,), (1,)), ((), ()))
VMEM_LIMIT = 56 * 1024 * 1024


def block_count(units, most):
    blocks = 1
    while units % blocks or units // blocks > most:
        blocks += 1
    return blocks


def exchange_kernel(
    units, pad, blocks, tokens, cot, ids, master,
    all_tokens, dense, spread, names,
    held, weights, packed, landed,
    held_sem, own_sem, row_sems, plane_sems, pair_sems, piece_sems, swap_sems, share_sems,
):
    groups, members = lax.axis_size("dp"), lax.axis_size("expert")
    pairs = members // 2
    count = groups * members
    group, member = lax.axis_index("dp"), lax.axis_index("expert")
    pair, half = member // 2, member % 2
    me = group * members + member
    own_rows, width = tokens.shape
    experts, top = master.shape[0], ids.shape[0]
    here = units // blocks
    group_rows = members * own_rows
    block_cols = master.shape[1] // blocks

    def device(g, e):
        return {"dp": g, "expert": e}

    def remote(source, target, sems, index, to):
        return pltpu.make_async_remote_copy(
            src_ref=source, dst_ref=target,
            send_sem=sems.at[(0, *index)], recv_sem=sems.at[(1, *index)],
            device_id=to, device_id_type=pl.DeviceIdType.MESH,
        )

    def shard(h, q, c):
        owner = ((group + groups - h) % groups) * members + 2 * ((pair + pairs - q) % pairs) + c
        return all_tokens.at[pl.ds(pl.multiple_of(owner * own_rows, own_rows), own_rows)]

    def along(h):
        to = device((group + h) % groups, member)
        return remote(shard(0, 0, half), shard(0, 0, half), row_sems, (h,), to)

    def across(h, q):
        to = device(group, 2 * ((pair + q) % pairs) + half)
        return remote(shard(h, 0, half), shard(h, 0, half), plane_sems, (h, q), to)

    def sideways(h, q):
        to = device(group, 2 * pair + 1 - half)
        return remote(shard(h, q, half), shard(h, q, half), pair_sems, (h, q), to)

    def piece(step):
        other = (me + step) % count
        source = packed.at[pl.ds(pl.multiple_of(other * pad, pad), pad)]
        target = landed.at[pl.ds(pl.multiple_of(me * pad, pad), pad)]
        return remote(source, target, piece_sems, (step,), device(other // members, other % members))

    share = 2 * units * top

    def part(h, q, c):
        owner = 2 * ((pair + pairs - q) % pairs) + c
        rows = pl.ds(pl.multiple_of(owner * share, share), share)
        return spread.at[(group + groups - h) % groups, rows]

    def swap(h, q):
        to = device(group, 2 * ((pair + q) % pairs) + half)
        return remote(part(h, 0, half), part(h, 0, half), swap_sems, (h, q), to)

    def pass_on(h, q):
        to = device(group, 2 * pair + 1 - half)
        return remote(part(h, q, half), part(h, q, half), share_sems, (h, q), to)

    loads = []
    for b in range(blocks):
        cols = pl.ds(b * block_cols, block_cols)
        loads.append(pltpu.make_async_copy(master.at[:, cols], held.at[:, cols], held_sem.at[b]))
    all_tokens[pl.ds(pl.multiple_of(me * own_rows, own_rows), own_rows), :] = tokens[...]

    barrier = pltpu.get_barrier_semaphore()

    @pl.loop(1, count)
    def _(step):
        other = (me + step) % count
        pl.semaphore_signal(
            barrier, inc=1, device_id=device(other // members, other % members),
            device_id_type=pl.DeviceIdType.MESH,
        )

    for load in loads:
        load.start()
    pl.semaphore_wait(barrier, count - 1)

    for h in range(1, groups):
        along(h).start()
    for q in range(1, pairs):
        across(0, q).start()
    sideways(0, 0).start()

    out_row = lax.broadcasted_iota(jnp.int32, (count * pad, cot.shape[1]), 0)
    in_col = lax.broadcasted_iota(jnp.int32, (count * pad, cot.shape[1]), 1)
    wanted = (out_row // pad) * units + out_row % pad
    pick = ((in_col == wanted) & (out_row % pad < units)).astype(jnp.bfloat16)
    turned_cot = lax.dot_general(pick, cot[...], NT, preferred_element_type=jnp.float32)
    lane = lax.broadcasted_iota(jnp.int32, (top, own_rows * top), 1)
    row = lax.broadcasted_iota(jnp.int32, (top, own_rows * top), 0)
    flat = jnp.zeros((top, own_rows * top), jnp.float32)
    numbers = ids[...].astype(jnp.float32)
    for t in range(own_rows):
        flat = flat + jnp.where(lane == t * top + row, numbers[:, t : t + 1], 0.0)
    flat = jnp.sum(flat, axis=0, keepdims=True)
    kind = lax.broadcasted_iota(jnp.int32, turned_cot.shape, 0) % pad
    packed[...] = jnp.where(kind == units, flat, turned_cot).astype(jnp.bfloat16)

    @pl.loop(1, count)
    def _(step):
        piece(step).start()

    mine = pl.ds(pl.multiple_of(me * pad, pad), pad)
    own = pltpu.make_async_copy(packed.at[mine], landed.at[mine], own_sem.at[0])
    own.start()

    for h in range(1, groups):
        along(h).wait_recv()
        for q in range(1, pairs):
            across(h, q).start()
        sideways(h, 0).start()

    for b in range(blocks):
        loads[b].wait()
        for c in range(2 * b * here, 2 * (b + 1) * here):
            weights[c * experts : (c + 1) * experts, :] = held[
                :, c * width : (c + 1) * width
            ].astype(jnp.bfloat16)

    own.wait()

    from_row = lax.broadcasted_iota(jnp.int32, (own_rows * top, group_rows), 0)
    to_col = lax.broadcasted_iota(jnp.int32, (own_rows * top, group_rows), 1) % own_rows
    source_row = lax.broadcasted_iota(jnp.int32, (members * pad, group_rows), 0) // pad
    source_col = lax.broadcasted_iota(jnp.int32, (members * pad, group_rows), 1) // own_rows
    same = (source_row == source_col).astype(jnp.float32)
    unit_row = lax.broadcasted_iota(jnp.int32, (pad, members * pad), 0)
    unit_col = lax.broadcasted_iota(jnp.int32, (pad, members * pad), 1) % pad
    gather = (unit_row == unit_col).astype(jnp.bfloat16)
    expert_row = lax.broadcasted_iota(jnp.int32, (experts, group_rows), 0).astype(jnp.float32)

    @pl.loop(0, groups)
    def _(h):
        now = (group + groups - h) % groups
        for q in range(1, pairs):
            across(h, q).wait_recv()
            sideways(h, q).start()
        for k in range(members):
            step = (me + count - (now * members + k)) % count

            @pl.when(step > 0)
            def _():
                piece(step).wait_recv()

        pieces = landed[pl.ds(pl.multiple_of(now * members * pad, members * pad), members * pad), :]
        turned = []
        for a in range(top):
            lanes = (from_row == to_col * top + a).astype(jnp.bfloat16)
            wide = jnp.dot(pieces, lanes, preferred_element_type=jnp.float32) * same
            turned.append(
                jnp.dot(gather, wide.astype(jnp.bfloat16), preferred_element_type=jnp.float32)
            )
        columns = pl.ds(pl.multiple_of(now * group_rows, group_rows), group_rows)
        names[:, columns] = jnp.concatenate([t[units : units + 1] for t in turned], axis=0)
        hot = [(t[units : units + 1] == expert_row).astype(jnp.float32) for t in turned]

        for q in range(pairs):
            sideways(h, q).wait_recv()
        group_tokens = all_tokens[columns, :]
        picked = []
        for b in range(blocks):
            first = b * (2 * here * experts)
            values = lax.dot_general(
                weights[first : first + 2 * here * experts, :],
                group_tokens,
                NT,
                preferred_element_type=jnp.float32,
            )
            both = []
            for u in range(here):
                gate = values[2 * u * experts : (2 * u + 1) * experts]
                up = values[(2 * u + 1) * experts : (2 * u + 2) * experts]
                unit = b * here + u
                cot_dense = turned[0][unit : unit + 1] * hot[0]
                for a in range(1, top):
                    cot_dense = cot_dense + turned[a][unit : unit + 1] * hot[a]
                sig = 1.0 / (1.0 + jnp.exp(-gate))
                d_gate = cot_dense * up * (sig * (1.0 + gate * (1.0 - sig)))
                d_up = cot_dense * (gate * sig)
                both += [d_gate, d_up]
                picked += [
                    jnp.sum(d * hot[a], axis=0, keepdims=True)
                    for d in (d_gate, d_up)
                    for a in range(top)
                ]
            dense[first : first + 2 * here * experts, columns] = jnp.concatenate(
                both, axis=0
            ).astype(jnp.bfloat16)
        rows = pl.ds(pl.multiple_of(member * share, share), share)
        spread[now, rows, :] = jnp.concatenate(picked, axis=0).astype(jnp.bfloat16)
        for q in range(1, pairs):
            swap(h, q).start()
        pass_on(h, 0).start()

        @pl.when(h > 0)
        def _():
            for q in range(1, pairs):
                swap(h - 1, q).wait_recv()
                pass_on(h - 1, q).start()

    for q in range(1, pairs):
        swap(groups - 1, q).wait_recv()
        pass_on(groups - 1, q).start()

    @pl.loop(1, count)
    def _(step):
        piece(step).wait_send()

    for h in range(groups):
        if h:
            along(h).wait_send()
        for q in range(pairs):
            if q:
                across(h, q).wait_send()
                swap(h, q).wait_send()
            sideways(h, q).wait_send()
            pass_on(h, q).wait()


def exchange(units, tokens, cotangent, expert_ids, master):
    groups, members = lax.axis_size("dp"), lax.axis_size("expert")
    count = groups * members
    own_rows, width = tokens.shape
    top, hidden = cotangent.shape[1:]
    total = own_rows * count
    experts = master.shape[0]
    pad = -(-(units + 1) // 16) * 16
    blocks = block_count(units, 3)
    dma = pltpu.SemaphoreType.DMA
    vmem = pl.BlockSpec(memory_space=pltpu.VMEM)
    return pl.pallas_call(
        functools.partial(exchange_kernel, units, pad, blocks),
        in_specs=[vmem, vmem, vmem, pl.BlockSpec(memory_space=pl.ANY)],
        out_specs=[vmem] * 4,
        out_shape=[
            jax.ShapeDtypeStruct((total, width), jnp.bfloat16),
            jax.ShapeDtypeStruct((2 * units * experts, total), jnp.bfloat16),
            jax.ShapeDtypeStruct((groups, members * 2 * units * top, members * own_rows), jnp.bfloat16),
            jax.ShapeDtypeStruct((top, total), jnp.float32),
        ],
        scratch_shapes=[
            pltpu.VMEM(master.shape, jnp.float32),
            pltpu.VMEM((2 * units * experts, width), jnp.bfloat16),
            pltpu.VMEM((count * pad, own_rows * top), jnp.bfloat16),
            pltpu.VMEM((count * pad, own_rows * top), jnp.bfloat16),
            dma((blocks,)),
            dma((1,)),
            dma((2, groups)),
            dma((2, groups, members // 2)),
            dma((2, groups, members // 2)),
            dma((2, count)),
            dma((2, groups, members // 2)),
            dma((2, groups, members // 2)),
        ],
        compiler_params=pltpu.CompilerParams(
            collective_id=0, has_side_effects=True, vmem_limit_bytes=VMEM_LIMIT
        ),
        name="exchange",
    )(tokens, cotangent.reshape(own_rows * top, hidden), expert_ids.T, master)


def finish_kernel(
    top, token_rows, placement, names, spread, dense, tokens, master, first, second,
    new_master, new_first, new_second, out, fold,
):
    experts = master.shape[0]
    width = tokens.shape[1]
    units = out.shape[1]
    groups, rows, group_rows = spread.shape

    @pl.when(pl.program_id(0) == 0)
    def _():
        out_row = lax.broadcasted_iota(jnp.int32, fold.shape, 0)
        in_row = lax.broadcasted_iota(jnp.int32, fold.shape, 1) // top
        wanted = (in_row % 2) * units + in_row // 2
        fold[...] = (out_row == wanted).astype(jnp.bfloat16)

    slot = lax.axis_index("expert") * pl.num_programs(0) + pl.program_id(0)
    expert = placement[slot]
    replicas, rank = jnp.int32(0), jnp.int32(0)
    for other in range(placement.shape[0]):
        equal = jnp.where(placement[other] == expert, 1, 0)
        replicas = replicas + equal
        rank = rank + jnp.where(other < slot, equal, 0)
    lane = lax.broadcasted_iota(jnp.int32, names.shape, 1)
    source = (lane // token_rows) % lax.axis_size("expert")
    chosen_source = lax.rem(source, jnp.full(source.shape, replicas)) == rank
    held = names[...] == expert.astype(jnp.float32)
    mask = jnp.where(held & chosen_source, 1.0, 0.0)
    both = jnp.concatenate([mask, mask], axis=0).astype(jnp.bfloat16)
    masked = jnp.concatenate(
        [
            (
                spread[g].reshape(rows // (2 * top), 2 * top, group_rows)
                * both[None, :, g * group_rows : (g + 1) * group_rows]
            ).reshape(rows, group_rows)
            for g in range(groups)
        ],
        axis=1,
    )
    chosen = jnp.dot(
        fold[...], masked, preferred_element_type=jnp.float32
    ).astype(jnp.bfloat16)
    grad = jnp.dot(chosen, tokens[...], preferred_element_type=jnp.float32)
    out[0, :, :width] = grad[:units]
    out[0, :, width:] = grad[units:]
    grads = jnp.dot(dense[...], tokens[...], preferred_element_type=jnp.float32)
    for c in range(master.shape[1] // width):
        cols = slice(c * width, (c + 1) * width)
        results = adamw_update(
            master[:, cols],
            first[:, cols],
            second[:, cols],
            grads[c * experts : (c + 1) * experts],
        )
        new_master[:, cols], new_first[:, cols], new_second[:, cols] = results


def finish(units, slots, token_rows, placement, names, spread, dense, tokens, master, first, second):
    top, total = names.shape
    experts, shard = master.shape
    width = tokens.shape[1]
    state = pl.BlockSpec((experts, shard // slots), lambda i: (0, i))
    return pl.pallas_call(
        functools.partial(finish_kernel, top, token_rows),
        grid=(slots,),
        in_specs=[
            pl.BlockSpec(memory_space=pltpu.SMEM),
            pl.BlockSpec(names.shape, lambda i: (0, 0)),
            pl.BlockSpec(spread.shape, lambda i: (0, 0, 0)),
            pl.BlockSpec((dense.shape[0] // slots, total), lambda i: (i, 0)),
            pl.BlockSpec(tokens.shape, lambda i: (0, 0)),
            state,
            state,
            state,
        ],
        out_specs=[state] * 3 + [pl.BlockSpec((1, units, 2 * width), lambda i: (i, 0, 0))],
        out_shape=[jax.ShapeDtypeStruct(master.shape, jnp.float32)] * 3
        + [jax.ShapeDtypeStruct((slots, units, 2 * width), jnp.float32)],
        scratch_shapes=[pltpu.VMEM((2 * units, spread.shape[1]), jnp.bfloat16)],
        compiler_params=pltpu.CompilerParams(
            dimension_semantics=("arbitrary",), vmem_limit_bytes=VMEM_LIMIT
        ),
        name="finish",
    )(placement, names, spread, dense, tokens, master, first, second)


def move_tokens(tokens, cotangent, expert_ids, placement, master, first_moment, second_moment):
    members = lax.axis_size("expert")
    units = master.shape[1] // (2 * tokens.shape[1])
    slot_local = placement.shape[0] // members
    all_tokens, dense, spread, names = exchange(units, tokens, cotangent, expert_ids, master)
    return tuple(
        finish(
            units * members, slot_local, tokens.shape[0], placement, names, spread, dense, all_tokens,
            master, first_moment, second_moment,
        )
    )


def local(tokens, cotangent, expert_ids, placement, master, first_moment, second_moment):
    devices = lax.axis_size("dp") * lax.axis_size("expert")
    token_values = tokens.size * devices
    weight_values = placement.shape[0] // lax.axis_size("expert") * cotangent.shape[2] * 2 * tokens.shape[1]
    whole_units = master.shape[1] % (2 * tokens.shape[1]) == 0
    few = token_values < weight_values and tokens.shape[0] * lax.axis_size("expert") % 128 == 0
    exact = master.shape[0] <= 256 and tokens.shape[0] % 16 == 0 and cotangent.shape[1] % 8 == 0
    slot_local = placement.shape[0] // lax.axis_size("expert")
    even = lax.axis_size("expert") % 2 == 0
    even = even and master.shape[1] // tokens.shape[1] % slot_local == 0
    plan = move_tokens if whole_units and few and exact and even else move_weights
    return plan(tokens, cotangent, expert_ids, placement, master, first_moment, second_moment)


def solution(mesh):
    return jax.shard_map(
        local,
        mesh=mesh,
        in_specs=(
            P(("dp", "expert"), None),
            P(("dp", "expert"), None, None),
            P(("dp", "expert"), None),
            P(),
            P(None, ("dp", "expert")),
            P(None, ("dp", "expert")),
            P(None, ("dp", "expert")),
        ),
        out_specs=(
            P(None, ("dp", "expert")),
            P(None, ("dp", "expert")),
            P(None, ("dp", "expert")),
            P("expert", "dp", None),
        ),
        check_vma=False,
    )
```

```python
import functools

import jax
import jax.numpy as jnp
from jax import lax
from jax.experimental import pallas as pl
from jax.experimental.pallas import tpu as pltpu
from jax.sharding import PartitionSpec as P

MOST = 5


beta_first = 0.9
beta_second = 0.95
learning_rate = 0.01
decay_rate = 0.1
epsilon = 1e-08
adam_steps = 20.0


def adamw_update(master, first_moment, second_moment, grads):
    new_first = beta_first * first_moment + (1.0 - beta_first) * grads
    new_second = beta_second * second_moment + (1.0 - beta_second) * grads * grads
    corr_first = 1.0 - beta_first**adam_steps
    corr_second = 1.0 - beta_second**adam_steps
    update = (
        new_first / corr_first / (jnp.sqrt(new_second / corr_second) + epsilon)
        + decay_rate * master
    )
    return (master - learning_rate * update, new_first, new_second)


def move_weights(tokens, cotangent, expert_ids, placement, master, first_moment, second_moment):
    expert_devices = lax.axis_size("expert")
    source_index = lax.axis_index("expert")
    slot_count = placement.shape[0]
    slot_local = slot_count // expert_devices
    expert_count = master.shape[0]
    shard_width = master.shape[1]
    token_rows = tokens.shape[0]
    model_width = tokens.shape[1]
    top_count = expert_ids.shape[1]
    hidden_width = cotangent.shape[2]
    assigned = token_rows * top_count
    piece_rows = shard_width * expert_devices // (2 * model_width)
    send_total = slot_count * MOST
    expert_range = jnp.arange(expert_count, dtype=jnp.int32)
    slot_range = jnp.arange(slot_count, dtype=jnp.int32)
    slot_hot = placement[:, None] == expert_range[None, :]
    replicas = jnp.sum(slot_hot.astype(jnp.int32), axis=0)
    earlier_same = (slot_range[:, None] > slot_range[None, :]) & (
        placement[:, None] == placement[None, :]
    )
    slot_rank = jnp.sum(earlier_same.astype(jnp.int32), axis=1)
    wanted = jnp.mod(source_index, replicas)
    target_hot = slot_hot & (slot_rank[:, None] == wanted[None, :])
    target_slot = jnp.sum(jnp.where(target_hot, slot_range[:, None], 0), axis=0)
    flat_ids = expert_ids.reshape(assigned)
    expert_hot = flat_ids[:, None] == expert_range[None, :]
    earlier = jnp.cumsum(expert_hot.astype(jnp.int32), axis=0) - 1
    position = jnp.sum(jnp.where(expert_hot, earlier, 0), axis=1)
    destination = jnp.sum(jnp.where(expert_hot, target_slot[None, :], 0), axis=1)
    target_device = destination // slot_local
    local_slot = destination % slot_local
    send_row = (local_slot * expert_devices + target_device) * MOST + position
    copy_range = jnp.arange(assigned, dtype=jnp.int32)
    row_match = jnp.arange(send_total, dtype=jnp.int32)[:, None] == send_row[None, :]
    filled = jnp.any(row_match, axis=1)
    source_copy = jnp.sum(jnp.where(row_match, copy_range[None, :], 0), axis=1)
    gathered_x = jnp.take(tokens, source_copy // top_count, axis=0)
    send_x = jnp.where(filled[:, None], gathered_x, jnp.zeros_like(gathered_x))
    send_x = send_x.reshape(slot_local, expert_devices, MOST, model_width)
    gathered_dh = jnp.take(cotangent.reshape(assigned, hidden_width), source_copy, axis=0)
    send_dh = jnp.where(filled[:, None], gathered_dh, jnp.zeros_like(gathered_dh))
    send_dh = send_dh.reshape(slot_local, expert_devices, MOST, hidden_width)
    piece_expert = placement.reshape(expert_devices, slot_local).T
    send_weight = master[piece_expert].astype(jnp.bfloat16)
    recv_weight = lax.all_to_all(send_weight, "expert", split_axis=1, concat_axis=1, tiled=True)
    recv_x, recv_dh = (
        lax.all_to_all(send_x, "expert", split_axis=1, concat_axis=1, tiled=True),
        lax.all_to_all(send_dh, "expert", split_axis=1, concat_axis=1, tiled=True),
    )
    rows_x = recv_x.reshape(slot_local, expert_devices * MOST, model_width)
    rows_dh = recv_dh.reshape(slot_local, expert_devices * MOST, hidden_width)
    own_piece = recv_weight.reshape(slot_local, piece_rows, 2 * model_width)
    replica = lax.all_gather(own_piece, "dp", axis=1, tiled=True)
    replica_split = replica.reshape(slot_local, hidden_width, 2, model_width)
    both_values = jnp.einsum(
        "lrd,lcgd->lrgc", rows_x, replica_split, preferred_element_type=jnp.float32
    )
    gate_value = both_values[:, :, 0, :]
    up_value = both_values[:, :, 1, :]
    sigmoid_value = jax.nn.sigmoid(gate_value)
    activation = gate_value * sigmoid_value
    derivative = sigmoid_value * (1.0 + gate_value * (1.0 - sigmoid_value))
    d_gate = (rows_dh * up_value * derivative).astype(jnp.bfloat16)
    d_up = (rows_dh * activation).astype(jnp.bfloat16)
    d_both = jnp.stack([d_gate, d_up], axis=2)
    grad_block = jnp.einsum("lrgc,lrd->clgd", d_both, rows_x, preferred_element_type=jnp.float32)
    summed_rows = lax.psum_scatter(
        grad_block.reshape(lax.axis_size("dp") * piece_rows, slot_local, 2 * model_width).astype(
            jnp.bfloat16
        ),
        "dp",
        scatter_dimension=0,
        tiled=True,
    ).astype(jnp.float32)
    replica_grad = jnp.swapaxes(summed_rows, 0, 1)
    outgoing = replica_grad.reshape(slot_local, expert_devices, shard_width)
    incoming = lax.all_to_all(
        outgoing.astype(jnp.bfloat16), "expert", split_axis=1, concat_axis=1, tiled=True
    ).astype(outgoing.dtype)
    by_slot = jnp.swapaxes(incoming, 0, 1).reshape(slot_count, shard_width)
    grads = jnp.dot(
        slot_hot.T.astype(jnp.float32),
        by_slot,
        precision=lax.Precision.HIGHEST,
        preferred_element_type=jnp.float32,
    )
    new_master, new_first, new_second = adamw_update(master, first_moment, second_moment, grads)
    return (new_master, new_first, new_second, replica_grad)


NT = (((1,), (1,)), ((), ()))
VMEM_LIMIT = 56 * 1024 * 1024


def block_count(units, most):
    blocks = 1
    while units % blocks or units // blocks > most:
        blocks += 1
    return blocks


def exchange_kernel(
    units, pad, blocks, tokens, cot, ids, master,
    all_tokens, dense, spread, names,
    held, weights, packed, landed,
    held_sem, own_sem, row_sems, plane_sems, pair_sems, piece_sems, swap_sems, share_sems,
):
    groups, members = lax.axis_size("dp"), lax.axis_size("expert")
    pairs = members // 2
    count = groups * members
    group, member = lax.axis_index("dp"), lax.axis_index("expert")
    pair, half = member // 2, member % 2
    me = group * members + member
    own_rows, width = tokens.shape
    experts, top = master.shape[0], ids.shape[0]
    here = units // blocks
    group_rows = members * own_rows
    block_cols = master.shape[1] // blocks

    def device(g, e):
        return {"dp": g, "expert": e}

    def remote(source, target, sems, index, to):
        return pltpu.make_async_remote_copy(
            src_ref=source, dst_ref=target,
            send_sem=sems.at[(0, *index)], recv_sem=sems.at[(1, *index)],
            device_id=to, device_id_type=pl.DeviceIdType.MESH,
        )

    relays = pairs == 4
    direct = [q for q in range(1, pairs) if not (relays and q == 2)]

    def order(place):
        return place + (place // 2) * (1 - 2 * (place % 2)) if relays else place

    def pair_at(offset):
        return order((order(pair) + offset) % pairs)

    def shard(h, q, c):
        owner = ((group + groups - h) % groups) * members + 2 * pair_at(pairs - q) + c
        return all_tokens.at[pl.ds(pl.multiple_of(owner * own_rows, own_rows), own_rows)]

    def along(h):
        to = device((group + h) % groups, member)
        return remote(shard(0, 0, half), shard(0, 0, half), row_sems, (h,), to)

    def across(h, q):
        to = device(group, 2 * pair_at(q) + half)
        return remote(shard(h, 0, half), shard(h, 0, half), plane_sems, (h, q), to)

    def relay(h):
        via = 1 + 2 * (h % 2)
        to = device(group, 2 * pair_at(via) + half)
        return remote(shard(h, via, half), shard(h, via, half), plane_sems, (h, 2), to)

    def arrived(h):
        for q in direct:
            across(h, q).wait_recv()
        if relays:
            relay(h).start()
        for q in direct:
            sideways(h, q).start()

    def sideways(h, q):
        to = device(group, 2 * pair + 1 - half)
        return remote(shard(h, q, half), shard(h, q, half), pair_sems, (h, q), to)

    def piece(step):
        other = (me + step) % count
        source = packed.at[pl.ds(pl.multiple_of(other * pad, pad), pad)]
        target = landed.at[pl.ds(pl.multiple_of(me * pad, pad), pad)]
        return remote(source, target, piece_sems, (step,), device(other // members, other % members))

    share = 2 * units * top

    def part(h, q, c):
        owner = 2 * pair_at(pairs - q) + c
        rows = pl.ds(pl.multiple_of(owner * share, share), share)
        return spread.at[(group + groups - h) % groups, rows]

    def swap(h, q):
        to = device(group, 2 * pair_at(q) + half)
        return remote(part(h, 0, half), part(h, 0, half), swap_sems, (h, q), to)

    def swap_relay(h):
        via = 1 + 2 * (h % 2)
        to = device(group, 2 * pair_at(via) + half)
        return remote(part(h, via, half), part(h, via, half), swap_sems, (h, 2), to)

    def swapped(h):
        for q in direct:
            swap(h, q).wait_recv()
        if relays:
            swap_relay(h).start()
        for q in direct:
            pass_on(h, q).start()

    def swapped_far(h):
        if relays:
            swap(h, 2).wait_recv()
            pass_on(h, 2).start()

    def pass_on(h, q):
        to = device(group, 2 * pair + 1 - half)
        return remote(part(h, q, half), part(h, q, half), share_sems, (h, q), to)

    loads = []
    for b in range(blocks):
        cols = pl.ds(b * block_cols, block_cols)
        loads.append(pltpu.make_async_copy(master.at[:, cols], held.at[:, cols], held_sem.at[b]))
    all_tokens[pl.ds(pl.multiple_of(me * own_rows, own_rows), own_rows), :] = tokens[...]

    barrier = pltpu.get_barrier_semaphore()

    @pl.loop(1, count)
    def _(step):
        other = (me + step) % count
        pl.semaphore_signal(
            barrier, inc=1, device_id=device(other // members, other % members),
            device_id_type=pl.DeviceIdType.MESH,
        )

    for load in loads:
        load.start()
    pl.semaphore_wait(barrier, count - 1)

    for h in range(1, groups):
        along(h).start()
    for q in direct:
        across(0, q).start()
    sideways(0, 0).start()

    out_row = lax.broadcasted_iota(jnp.int32, (count * pad, cot.shape[1]), 0)
    in_col = lax.broadcasted_iota(jnp.int32, (count * pad, cot.shape[1]), 1)
    wanted = (out_row // pad) * units + out_row % pad
    pick = ((in_col == wanted) & (out_row % pad < units)).astype(jnp.bfloat16)
    turned_cot = lax.dot_general(pick, cot[...], NT, preferred_element_type=jnp.float32)
    lane = lax.broadcasted_iota(jnp.int32, (top, own_rows * top), 1)
    row = lax.broadcasted_iota(jnp.int32, (top, own_rows * top), 0)
    flat = jnp.zeros((top, own_rows * top), jnp.float32)
    numbers = ids[...].astype(jnp.float32)
    for t in range(own_rows):
        flat = flat + jnp.where(lane == t * top + row, numbers[:, t : t + 1], 0.0)
    flat = jnp.sum(flat, axis=0, keepdims=True)
    kind = lax.broadcasted_iota(jnp.int32, turned_cot.shape, 0) % pad
    packed[...] = jnp.where(kind == units, flat, turned_cot).astype(jnp.bfloat16)

    @pl.loop(1, count)
    def _(step):
        piece(step).start()

    mine = pl.ds(pl.multiple_of(me * pad, pad), pad)
    own = pltpu.make_async_copy(packed.at[mine], landed.at[mine], own_sem.at[0])
    own.start()

    for h in range(1, groups):
        along(h).wait_recv()
        for q in direct:
            across(h, q).start()
        sideways(h, 0).start()

    arrived(0)
    for b in range(blocks):
        loads[b].wait()
        for c in range(2 * b * here, 2 * (b + 1) * here):
            weights[c * experts : (c + 1) * experts, :] = held[
                :, c * width : (c + 1) * width
            ].astype(jnp.bfloat16)

    own.wait()

    from_row = lax.broadcasted_iota(jnp.int32, (own_rows * top, group_rows), 0)
    to_col = lax.broadcasted_iota(jnp.int32, (own_rows * top, group_rows), 1) % own_rows
    source_row = lax.broadcasted_iota(jnp.int32, (members * pad, group_rows), 0) // pad
    source_col = lax.broadcasted_iota(jnp.int32, (members * pad, group_rows), 1) // own_rows
    same = (source_row == source_col).astype(jnp.float32)
    unit_row = lax.broadcasted_iota(jnp.int32, (pad, members * pad), 0)
    unit_col = lax.broadcasted_iota(jnp.int32, (pad, members * pad), 1) % pad
    gather = (unit_row == unit_col).astype(jnp.bfloat16)
    expert_row = lax.broadcasted_iota(jnp.int32, (experts, group_rows), 0).astype(jnp.float32)

    @pl.loop(0, groups)
    def _(h):
        now = (group + groups - h) % groups
        if relays:
            across(h, 2).wait_recv()
            sideways(h, 2).start()

        @pl.when(h < groups - 1)
        def _():
            arrived(h + 1)

        for k in range(members):
            step = (me + count - (now * members + k)) % count

            @pl.when(step > 0)
            def _():
                piece(step).wait_recv()

        pieces = landed[pl.ds(pl.multiple_of(now * members * pad, members * pad), members * pad), :]
        turned = []
        for a in range(top):
            lanes = (from_row == to_col * top + a).astype(jnp.bfloat16)
            wide = jnp.dot(pieces, lanes, preferred_element_type=jnp.float32) * same
            turned.append(
                jnp.dot(gather, wide.astype(jnp.bfloat16), preferred_element_type=jnp.float32)
            )
        columns = pl.ds(pl.multiple_of(now * group_rows, group_rows), group_rows)
        names[:, columns] = jnp.concatenate([t[units : units + 1] for t in turned], axis=0)
        hot = [(t[units : units + 1] == expert_row).astype(jnp.float32) for t in turned]

        for q in range(pairs):
            sideways(h, q).wait_recv()
        group_tokens = all_tokens[columns, :]
        picked = []
        for b in range(blocks):
            first = b * (2 * here * experts)
            values = lax.dot_general(
                weights[first : first + 2 * here * experts, :],
                group_tokens,
                NT,
                preferred_element_type=jnp.float32,
            )
            both = []
            for u in range(here):
                gate = values[2 * u * experts : (2 * u + 1) * experts]
                up = values[(2 * u + 1) * experts : (2 * u + 2) * experts]
                unit = b * here + u
                cot_dense = turned[0][unit : unit + 1] * hot[0]
                for a in range(1, top):
                    cot_dense = cot_dense + turned[a][unit : unit + 1] * hot[a]
                sig = 1.0 / (1.0 + jnp.exp(-gate))
                d_gate = cot_dense * up * (sig * (1.0 + gate * (1.0 - sig)))
                d_up = cot_dense * (gate * sig)
                both += [d_gate, d_up]
                picked += [
                    jnp.sum(d * hot[a], axis=0, keepdims=True)
                    for d in (d_gate, d_up)
                    for a in range(top)
                ]
            dense[first : first + 2 * here * experts, columns] = jnp.concatenate(
                both, axis=0
            ).astype(jnp.bfloat16)
        rows = pl.ds(pl.multiple_of(member * share, share), share)
        spread[now, rows, :] = jnp.concatenate(picked, axis=0).astype(jnp.bfloat16)
        for q in direct:
            swap(h, q).start()
        pass_on(h, 0).start()

        @pl.when(h > 0)
        def _():
            swapped(h - 1)

        @pl.when(h > 1)
        def _():
            swapped_far(h - 2)

    swapped(groups - 1)
    for h in range(max(groups - 2, 0), groups):
        swapped_far(h)

    @pl.loop(1, count)
    def _(step):
        piece(step).wait_send()

    for h in range(groups):
        if h:
            along(h).wait_send()
        for q in range(pairs):
            if q in direct:
                across(h, q).wait_send()
                swap(h, q).wait_send()
            elif q:
                relay(h).wait_send()
                swap_relay(h).wait_send()
            sideways(h, q).wait_send()
            pass_on(h, q).wait()


def exchange(units, tokens, cotangent, expert_ids, master):
    groups, members = lax.axis_size("dp"), lax.axis_size("expert")
    count = groups * members
    own_rows, width = tokens.shape
    top, hidden = cotangent.shape[1:]
    total = own_rows * count
    experts = master.shape[0]
    pad = -(-(units + 1) // 16) * 16
    blocks = block_count(units, 3)
    dma = pltpu.SemaphoreType.DMA
    vmem = pl.BlockSpec(memory_space=pltpu.VMEM)
    return pl.pallas_call(
        functools.partial(exchange_kernel, units, pad, blocks),
        in_specs=[vmem, vmem, vmem, pl.BlockSpec(memory_space=pl.ANY)],
        out_specs=[vmem] * 4,
        out_shape=[
            jax.ShapeDtypeStruct((total, width), jnp.bfloat16),
            jax.ShapeDtypeStruct((2 * units * experts, total), jnp.bfloat16),
            jax.ShapeDtypeStruct((groups, members * 2 * units * top, members * own_rows), jnp.bfloat16),
            jax.ShapeDtypeStruct((top, total), jnp.float32),
        ],
        scratch_shapes=[
            pltpu.VMEM(master.shape, jnp.float32),
            pltpu.VMEM((2 * units * experts, width), jnp.bfloat16),
            pltpu.VMEM((count * pad, own_rows * top), jnp.bfloat16),
            pltpu.VMEM((count * pad, own_rows * top), jnp.bfloat16),
            dma((blocks,)),
            dma((1,)),
            dma((2, groups)),
            dma((2, groups, members // 2)),
            dma((2, groups, members // 2)),
            dma((2, count)),
            dma((2, groups, members // 2)),
            dma((2, groups, members // 2)),
        ],
        compiler_params=pltpu.CompilerParams(
            collective_id=0, has_side_effects=True, vmem_limit_bytes=VMEM_LIMIT
        ),
        name="exchange",
    )(tokens, cotangent.reshape(own_rows * top, hidden), expert_ids.T, master)


def finish_kernel(
    top, token_rows, placement, names, spread, dense, tokens, master, first, second,
    new_master, new_first, new_second, out, fold,
):
    experts = master.shape[0]
    width = tokens.shape[1]
    units = out.shape[1]
    groups, rows, group_rows = spread.shape

    @pl.when(pl.program_id(0) == 0)
    def _():
        out_row = lax.broadcasted_iota(jnp.int32, fold.shape, 0)
        in_row = lax.broadcasted_iota(jnp.int32, fold.shape, 1) // top
        wanted = (in_row % 2) * units + in_row // 2
        fold[...] = (out_row == wanted).astype(jnp.bfloat16)

    slot = lax.axis_index("expert") * pl.num_programs(0) + pl.program_id(0)
    expert = placement[slot]
    replicas, rank = jnp.int32(0), jnp.int32(0)
    for other in range(placement.shape[0]):
        equal = jnp.where(placement[other] == expert, 1, 0)
        replicas = replicas + equal
        rank = rank + jnp.where(other < slot, equal, 0)
    lane = lax.broadcasted_iota(jnp.int32, names.shape, 1)
    source = (lane // token_rows) % lax.axis_size("expert")
    chosen_source = lax.rem(source, jnp.full(source.shape, replicas)) == rank
    held = names[...] == expert.astype(jnp.float32)
    mask = jnp.where(held & chosen_source, 1.0, 0.0)
    both = jnp.concatenate([mask, mask], axis=0).astype(jnp.bfloat16)
    masked = jnp.concatenate(
        [
            (
                spread[g].reshape(rows // (2 * top), 2 * top, group_rows)
                * both[None, :, g * group_rows : (g + 1) * group_rows]
            ).reshape(rows, group_rows)
            for g in range(groups)
        ],
        axis=1,
    )
    chosen = jnp.dot(
        fold[...], masked, preferred_element_type=jnp.float32
    ).astype(jnp.bfloat16)
    grad = jnp.dot(chosen, tokens[...], preferred_element_type=jnp.float32)
    out[0, :, :width] = grad[:units]
    out[0, :, width:] = grad[units:]
    grads = jnp.dot(dense[...], tokens[...], preferred_element_type=jnp.float32)
    for c in range(master.shape[1] // width):
        cols = slice(c * width, (c + 1) * width)
        results = adamw_update(
            master[:, cols],
            first[:, cols],
            second[:, cols],
            grads[c * experts : (c + 1) * experts],
        )
        new_master[:, cols], new_first[:, cols], new_second[:, cols] = results


def finish(units, slots, token_rows, placement, names, spread, dense, tokens, master, first, second):
    top, total = names.shape
    experts, shard = master.shape
    width = tokens.shape[1]
    state = pl.BlockSpec((experts, shard // slots), lambda i: (0, i))
    return pl.pallas_call(
        functools.partial(finish_kernel, top, token_rows),
        grid=(slots,),
        in_specs=[
            pl.BlockSpec(memory_space=pltpu.SMEM),
            pl.BlockSpec(names.shape, lambda i: (0, 0)),
            pl.BlockSpec(spread.shape, lambda i: (0, 0, 0)),
            pl.BlockSpec((dense.shape[0] // slots, total), lambda i: (i, 0)),
            pl.BlockSpec(tokens.shape, lambda i: (0, 0)),
            state,
            state,
            state,
        ],
        out_specs=[state] * 3 + [pl.BlockSpec((1, units, 2 * width), lambda i: (i, 0, 0))],
        out_shape=[jax.ShapeDtypeStruct(master.shape, jnp.float32)] * 3
        + [jax.ShapeDtypeStruct((slots, units, 2 * width), jnp.float32)],
        scratch_shapes=[pltpu.VMEM((2 * units, spread.shape[1]), jnp.bfloat16)],
        compiler_params=pltpu.CompilerParams(
            dimension_semantics=("arbitrary",), vmem_limit_bytes=VMEM_LIMIT
        ),
        name="finish",
    )(placement, names, spread, dense, tokens, master, first, second)


def move_tokens(tokens, cotangent, expert_ids, placement, master, first_moment, second_moment):
    members = lax.axis_size("expert")
    units = master.shape[1] // (2 * tokens.shape[1])
    slot_local = placement.shape[0] // members
    all_tokens, dense, spread, names = exchange(units, tokens, cotangent, expert_ids, master)
    return tuple(
        finish(
            units * members, slot_local, tokens.shape[0], placement, names, spread, dense, all_tokens,
            master, first_moment, second_moment,
        )
    )


def local(tokens, cotangent, expert_ids, placement, master, first_moment, second_moment):
    devices = lax.axis_size("dp") * lax.axis_size("expert")
    token_values = tokens.size * devices
    weight_values = placement.shape[0] // lax.axis_size("expert") * cotangent.shape[2] * 2 * tokens.shape[1]
    whole_units = master.shape[1] % (2 * tokens.shape[1]) == 0
    few = token_values < weight_values and tokens.shape[0] * lax.axis_size("expert") % 128 == 0
    exact = master.shape[0] <= 256 and tokens.shape[0] % 16 == 0 and cotangent.shape[1] % 8 == 0
    slot_local = placement.shape[0] // lax.axis_size("expert")
    even = lax.axis_size("expert") % 2 == 0
    even = even and master.shape[1] // tokens.shape[1] % slot_local == 0
    plan = move_tokens if whole_units and few and exact and even else move_weights
    return plan(tokens, cotangent, expert_ids, placement, master, first_moment, second_moment)


def solution(mesh):
    return jax.shard_map(
        local,
        mesh=mesh,
        in_specs=(
            P(("dp", "expert"), None),
            P(("dp", "expert"), None, None),
            P(("dp", "expert"), None),
            P(),
            P(None, ("dp", "expert")),
            P(None, ("dp", "expert")),
            P(None, ("dp", "expert")),
        ),
        out_specs=(
            P(None, ("dp", "expert")),
            P(None, ("dp", "expert")),
            P(None, ("dp", "expert")),
            P("expert", "dp", None),
        ),
        check_vma=False,
    )
```
